256 devices in a mesh: dp: 32 (over y, z), mp: 8 (over x, core).
Axes of the slice: x: 4, y: 4, z: 8, core: 2. Of those that a mesh axis runs over, the one named last changes fastest.
Arguments:
- grads: bfloat16 [768, 512, 512], P('dp', 'mp'), may hold values from -6 to 6
- owner_slot: int32 [768], P('dp'), may hold values from 0 to 767, as said below
- refresh_flag: int32 [768], P(('dp', 'mp')), may hold values from 0 to 1, as said below
- left_stats: bfloat16 [768, 512, 512], P(('dp', 'mp')), may hold values from -1 to 16, as said below
- right_stats: bfloat16 [768, 512, 512], P(('dp', 'mp')), may hold values from -1 to 16, as said below
- left_root: bfloat16 [768, 512, 512], P(('dp', 'mp')), may hold values from -1 to 1, as said below
- right_root: bfloat16 [768, 512, 512], P(('dp', 'mp')), may hold values from -1 to 1, as said below
Outputs:
- left_new: bfloat16 [768, 512, 512], P(('dp', 'mp'))
- right_new: bfloat16 [768, 512, 512], P(('dp', 'mp'))
- direction: bfloat16 [768, 512, 512], P(('dp', 'mp'))
The draws below stay inside these ranges and needn't reach their ends.
Inputs may be any that keep to these rules, and one draw needn't show every extreme that they name: `owner_slot`: A permutation of the slots. Slot s lies on the device that is number s // 3 in dp-major order. The 24 blocks of one dp index go to exactly 2 slots of each owner dp index s // 24 that they reach, and each owner dp index receives exactly 24 blocks. Every dp index d sends blocks to the owner dp indices d + 1 and d + 16, counted round. `refresh_flag`: exactly 48 ones; at most one on a device, and at most one on the two devices with mp indices 2i and 2i + 1 of one dp index. `left_stats`: each block symmetric positive definite. `right_stats`: each block symmetric positive definite. `left_root`: each block symmetric positive definite. `right_root`: each block symmetric positive definite.
All inputs are finite; a program needn't handle non-finite values.
Results may differ from the reference program's by a relative error of at most 0.0051.
Values may be sent and summed in bfloat16 or wider, within the bound.
A program may use at most 64 MiB of HBM per device.

```python
import math
import jax
import jax.numpy as jnp
from jax import lax

B = 512
K = 3
CAP = 2
ITERS = 3
HB = 24
NBLK = 768
NREF = 48
DEVICES = 256


def dominant(key, low_diag, high_diag, low_kernel, high_kernel):
    key_diag, key_kernel, key_points = jax.random.split(key, 3)
    diagonal = jnp.exp(jax.random.uniform(key_diag, (NBLK, B), jnp.float32, math.log(low_diag), math.log(high_diag)))
    weight = jnp.sqrt(jnp.exp(jax.random.uniform(key_kernel, (NBLK, B), jnp.float32, math.log(low_kernel), math.log(high_kernel))))
    cube_side = float(B) ** (1.0 / 3.0)
    points = jax.random.uniform(key_points, (NBLK, B, 3), jnp.float32, 0.0, cube_side)
    squared = jnp.zeros((NBLK, B, B), jnp.float32)
    for coordinate in range(3):
        spacing = points[:, :, None, coordinate] - points[:, None, :, coordinate]
        squared = squared + spacing * spacing
    kernel = weight[:, :, None] * weight[:, None, :] * jnp.exp(-squared)
    identity = jnp.eye(B, dtype=jnp.float32)
    return kernel + identity * diagonal[:, :, None]


def draw_left_stats(key, part):
    key = jax.random.fold_in(key, 3)
    return dominant(key, 1.0, 6.0, 0.5, 4.0).astype(jnp.bfloat16)


def draw_right_stats(key, part):
    key = jax.random.fold_in(key, 5)
    return dominant(key, 1.0, 6.0, 0.5, 4.0).astype(jnp.bfloat16)


def draw_left_root(key, part):
    key = jax.random.fold_in(key, 7)
    return dominant(key, 0.3, 0.55, 0.1, 0.4).astype(jnp.bfloat16)


def draw_right_root(key, part):
    key = jax.random.fold_in(key, 9)
    return dominant(key, 0.3, 0.55, 0.1, 0.4).astype(jnp.bfloat16)


def draw_grads(key, part):
    key = jax.random.fold_in(key, 11)
    key_noise, key_rows, key_cols = jax.random.split(key, 3)
    noise = jnp.clip(jax.random.normal(key_noise, (NBLK, B, B), jnp.float32), -4.0, 4.0)
    top_scale = 10.0
    row_scale = jnp.exp(jax.random.uniform(key_rows, (NBLK, B, 1), jnp.float32, 0.0, math.log(top_scale)))
    col_scale = jnp.exp(jax.random.uniform(key_cols, (NBLK, 1, B), jnp.float32, 0.0, math.log(top_scale)))
    return (0.012 * noise * row_scale * col_scale).astype(jnp.bfloat16)


def draw_owner_slot(key, part):
    key = jax.random.fold_in(key, 37)
    key_offsets, key_holders, key_groups = jax.random.split(key, 3)
    owners = NBLK // HB
    shuffled = jax.random.permutation(key_offsets, owners).astype(jnp.int32)
    places = jnp.arange(owners, dtype=jnp.int32)
    ranked = jnp.where(shuffled == 1, -2, jnp.where(shuffled == owners // 2, -1, places))
    order = jnp.argsort(ranked, stable=True)
    offsets = shuffled[order][:HB // CAP]
    holder_perm = jax.vmap(lambda single: jax.random.permutation(single, HB))(jax.random.split(key_holders, owners))
    group_perm = jax.vmap(lambda single: jax.random.permutation(single, HB))(jax.random.split(key_groups, owners))
    pair_index = holder_perm // CAP
    holder_index = jnp.arange(owners, dtype=jnp.int32)[:, None]
    target = (holder_index + offsets[pair_index]) % owners
    local_slot = group_perm[target, holder_perm]
    return (target * HB + local_slot).reshape(NBLK).astype(jnp.int32)


def draw_refresh_flag(key, part):
    key = jax.random.fold_in(key, 23)
    key_pairs, key_member, key_slot = jax.random.split(key, 3)
    pair_count = DEVICES // 2
    chosen = jax.random.permutation(key_pairs, pair_count)[:NREF]
    member = jax.random.randint(key_member, (NREF,), 0, 2)
    inside = jax.random.randint(key_slot, (NREF,), 0, K)
    slot_index = (chosen * 2 + member) * K + inside
    return jnp.zeros((NBLK,), jnp.int32).at[slot_index].set(1)


def setup_inputs(seed: int = 0) -> dict:
    key_list = jax.random.split(jax.random.key(seed), 8)
    return {
        "grads": draw_grads(jax.random.fold_in(key_list[7], 71), 0),
        "owner_slot": draw_owner_slot(jax.random.fold_in(key_list[7], 71), 0),
        "refresh_flag": draw_refresh_flag(jax.random.fold_in(key_list[7], 71), 0),
        "left_stats": draw_left_stats(jax.random.fold_in(key_list[7], 71), 0),
        "right_stats": draw_right_stats(jax.random.fold_in(key_list[7], 71), 0),
        "left_root": draw_left_root(jax.random.fold_in(key_list[7], 71), 0),
        "right_root": draw_right_root(jax.random.fold_in(key_list[7], 71), 0),
    }


highest = lax.Precision.HIGHEST
decay_rate = 0.9

def inverse_root(matrix):
    identity = jnp.eye(B, dtype=jnp.float32)
    scaling = 2.5 / jnp.sqrt(jnp.sum(matrix * matrix) + 1e-06)
    current = scaling * matrix
    root_now = identity
    for iteration in range(ITERS):
        factor = (5.0 * identity - current) * 0.25
        if iteration == 0:
            root_now = scaling ** 0.25 * factor
        else:
            root_now = jnp.dot(root_now, factor, precision=highest)
        if iteration + 1 < ITERS:
            square = jnp.dot(factor, factor, precision=highest)
            fourth = jnp.dot(square, square, precision=highest)
            current = jnp.dot(fourth, current, precision=highest)
    return root_now.astype(jnp.bfloat16)

def statistics(block, left_old, right_old):
    gram_left = jnp.dot(block, block.T, preferred_element_type=jnp.float32)
    gram_right = jnp.dot(block.T, block, preferred_element_type=jnp.float32)
    left_next = (decay_rate * left_old.astype(jnp.float32) + (1.0 - decay_rate) * gram_left).astype(jnp.bfloat16)
    right_next = (decay_rate * right_old.astype(jnp.float32) + (1.0 - decay_rate) * gram_right).astype(jnp.bfloat16)
    return (left_next, right_next)

def reference(grads, owner_slot, refresh_flag, left_stats, right_stats, left_root, right_root):
    holder = jnp.zeros((NBLK,), jnp.int32).at[owner_slot].set(jnp.arange(NBLK, dtype=jnp.int32))
    chosen = jnp.nonzero(refresh_flag, size=NREF)[0].astype(jnp.int32)

    def refresh(slot_index):
        block = grads[holder[slot_index]]
        left_next, right_next = statistics(block, left_stats[slot_index], right_stats[slot_index])
        return (inverse_root(left_next.astype(jnp.float32)), inverse_root(right_next.astype(jnp.float32)))
    fresh_left, fresh_right = lax.map(refresh, chosen)
    left_use = left_root.at[chosen].set(fresh_left)
    right_use = right_root.at[chosen].set(fresh_right)

    def precondition(slot_index):
        block = grads[holder[slot_index]]
        left_next, right_next = statistics(block, left_stats[slot_index], right_stats[slot_index])
        half_way = jnp.dot(left_use[slot_index], block, preferred_element_type=jnp.float32).astype(jnp.bfloat16)
        preconditioned = jnp.dot(half_way, right_use[slot_index], preferred_element_type=jnp.float32)
        grad_norm = jnp.sum(jnp.square(block.astype(jnp.float32)))
        dir_norm = jnp.sum(preconditioned * preconditioned)
        grafted = (preconditioned * jnp.sqrt(grad_norm / (dir_norm + 1e-06))).astype(jnp.bfloat16)
        return (left_next, right_next, grafted)
    left_new, right_new, direction = lax.map(precondition, jnp.arange(NBLK, dtype=jnp.int32))
    return (left_new, right_new, direction)
```

```python
import jax
import jax.numpy as jnp
from jax import lax
from jax.experimental import pallas as pl
from jax.experimental.pallas import tpu as pltpu
from jax.sharding import PartitionSpec as P

CAP = 2

decay_rate = 0.9


def multiply(first_op, second_op):
    return jnp.dot(first_op, second_op, preferred_element_type=jnp.float32)


def newton_root(matrix):
    size = matrix.shape[0]
    identity = (
        lax.broadcasted_iota(jnp.int32, (size, size), 0) == lax.broadcasted_iota(jnp.int32, (size, size), 1)
    ).astype(jnp.float32)
    wide = matrix.astype(jnp.float32)
    scaling = 2.5 / jnp.sqrt(jnp.sum(wide * wide) + 1e-06)
    scaled = scaling * wide
    squared = (scaling * scaling) * multiply(matrix, matrix)
    shift = (squared - 10.0 * scaled) * 0.0625
    half_shift = shift.astype(jnp.bfloat16)
    quartic = 3.125 * shift + multiply(half_shift, half_shift)
    through = (5.0 * scaled - squared) * 0.25
    fifth = 2.44140625 * through + multiply(quartic.astype(jnp.bfloat16), through.astype(jnp.bfloat16))
    offset = -0.3125 * scaled - 0.25 * fifth
    half_offset = offset.astype(jnp.bfloat16)
    doubled = 3.125 * offset + multiply(half_offset, half_offset)
    half_doubled = doubled.astype(jnp.bfloat16)
    fourth = 4.8828125 * doubled + multiply(half_doubled, half_doubled)
    carried = 1.5625 * scaled + scaling * multiply(half_offset, matrix)
    last = 5.9604644775390625 * carried + multiply(fourth.astype(jnp.bfloat16), carried.astype(jnp.bfloat16))
    root = 1.953125 * identity + 1.25 * offset - 0.25 * last
    return (jnp.sqrt(jnp.sqrt(scaling)) * root).astype(jnp.bfloat16)


def update_kernel(flag_ref, grad_ref, left_ref, right_ref, left_root_ref, right_root_ref, left_out, right_out, dir_out, use_left, use_right):
    slot = pl.program_id(0)
    block = grad_ref[0]
    gram_left = lax.dot_general(block, block, (((1,), (1,)), ((), ())), preferred_element_type=jnp.float32)
    left_out[0] = (decay_rate * left_ref[0].astype(jnp.float32) + (1.0 - decay_rate) * gram_left).astype(jnp.bfloat16)
    gram_right = lax.dot_general(block, block, (((0,), (0,)), ((), ())), preferred_element_type=jnp.float32)
    right_out[0] = (decay_rate * right_ref[0].astype(jnp.float32) + (1.0 - decay_rate) * gram_right).astype(jnp.bfloat16)

    @pl.when(flag_ref[slot] > 0)
    def _():
        use_left[...] = newton_root(left_out[0])
        use_right[...] = newton_root(right_out[0])

    @pl.when(flag_ref[slot] <= 0)
    def _():
        use_left[...] = left_root_ref[0]
        use_right[...] = right_root_ref[0]

    half_way = multiply(use_left[...], block).astype(jnp.bfloat16)
    preconditioned = multiply(half_way, use_right[...])
    wide = block.astype(jnp.float32)
    grad_norm = jnp.sum(wide * wide)
    dir_norm = jnp.sum(preconditioned * preconditioned)
    dir_out[0] = (preconditioned * jnp.sqrt(grad_norm / (dir_norm + 1e-06))).astype(jnp.bfloat16)


def update(refresh_flag, blocks, left_stats, right_stats, left_root, right_root):
    slots, size = blocks.shape[0], blocks.shape[1]
    spec = pl.BlockSpec((1, size, size), lambda k: (k, 0, 0))
    return pl.pallas_call(
        update_kernel,
        grid=(slots,),
        in_specs=[pl.BlockSpec(memory_space=pltpu.SMEM)] + [spec] * 5,
        out_specs=[spec] * 3,
        out_shape=[jax.ShapeDtypeStruct(blocks.shape, jnp.bfloat16)] * 3,
        scratch_shapes=[pltpu.VMEM((size, size), jnp.bfloat16)] * 2,
        compiler_params=pltpu.CompilerParams(vmem_limit_bytes=56 << 20),
        name="update",
    )(refresh_flag, blocks, left_stats, right_stats, left_root, right_root)


def local(grads, owner_slot, refresh_flag, left_stats, right_stats, left_root, right_root):
    held_blocks = grads.shape[0]
    owners = lax.axis_size("dp")
    sending = owners * CAP
    target_owner = owner_slot // held_blocks
    within = owner_slot % held_blocks
    positions = jnp.arange(held_blocks, dtype=jnp.int32)
    earlier = (target_owner[None, :] == target_owner[:, None]) & (
        positions[None, :] < positions[:, None]
    )
    ranking = jnp.sum(earlier.astype(jnp.int32), axis=1)
    address = target_owner * CAP + ranking
    placing = jnp.arange(sending, dtype=jnp.int32)[:, None] == address[None, :]
    outgoing = jnp.einsum(
        "eh,hrc->erc", placing.astype(jnp.bfloat16), grads, preferred_element_type=jnp.float32
    ).astype(jnp.bfloat16)
    labels = jnp.sum(jnp.where(placing, within[None, :] + 1, 0), axis=1)
    send_shape = (owners, CAP) + grads.shape[1:]
    incoming, arrived_labels = (
        lax.all_to_all(outgoing.reshape(send_shape), "dp", split_axis=0, concat_axis=0, tiled=True),
        lax.all_to_all(labels.reshape(owners, CAP), "dp", split_axis=0, concat_axis=0, tiled=True),
    )
    incoming = incoming.reshape((sending,) + grads.shape[1:])
    arrived_labels = arrived_labels.reshape(sending)
    sorting = jnp.arange(held_blocks, dtype=jnp.int32)[:, None] == arrived_labels[None, :] - 1
    gathered = jnp.einsum(
        "qe,erc->qrc", sorting.astype(jnp.bfloat16), incoming, preferred_element_type=jnp.float32
    ).astype(jnp.bfloat16)
    blocks = lax.all_to_all(gathered, "mp", split_axis=0, concat_axis=1, tiled=True)
    return tuple(update(refresh_flag, blocks, left_stats, right_stats, left_root, right_root))


def solution(mesh):
    placed = (
        P("dp", "mp", None),
        P("dp"),
        P(("dp", "mp")),
        P(("dp", "mp"), None, None),
        P(("dp", "mp"), None, None),
        P(("dp", "mp"), None, None),
        P(("dp", "mp"), None, None),
    )
    return jax.shard_map(
        local,
        mesh=mesh,
        in_specs=placed,
        out_specs=(
            P(("dp", "mp"), None, None),
            P(("dp", "mp"), None, None),
            P(("dp", "mp"), None, None),
        ),
        check_vma=False,
    )
```

```python
import functools

import jax
import jax.numpy as jnp
from jax import lax
from jax.experimental import pallas as pl
from jax.experimental.pallas import tpu as pltpu
from jax.sharding import PartitionSpec as P

decay_rate = 0.9


def multiply(first_op, second_op):
    return jnp.dot(first_op, second_op, preferred_element_type=jnp.float32)


def iota2(shape, axis):
    return lax.broadcasted_iota(jnp.int32, shape, axis)


def total_of(mask, values):
    return jnp.max(jnp.where(mask, values, 0), keepdims=True)


def long_need(ones, twos, threes, fours):
    odd = twos & 1
    rest = jnp.maximum(ones - threes - 2 * odd, 0)
    lanes = fours + threes + ((twos + 1) >> 1) + ((rest + 3) >> 2)
    spare = ones - threes
    used = jnp.where(
        rest > 0,
        jnp.where((rest & 3) == 0, 4, rest & 3),
        jnp.where(
            twos > 0,
            jnp.where(odd == 1, 2 + jnp.clip(spare, 0, 2), 4),
            jnp.where(threes > 0, jnp.where(spare >= 0, 4, 3), 4),
        ),
    )
    return jnp.where(lanes > 0, 4 * (lanes - 1) + used, 0)


def long_plan(counts, hop, rank):
    n1, n2, n3, n4, n5, n6, n7 = counts
    best, split = long_need(n1, n2, n3, 0 * n4), 0 * n4
    best = jnp.maximum(best, long_need(n7, n6, n5, n4))
    for c in range(1, 5):
        other = jnp.maximum(long_need(n1, n2, n3, 0 * n4 + c), long_need(n7, n6, n5, jnp.maximum(n4 - c, 0)))
        better = (n4 >= c) & (other < best)
        best, split = jnp.where(better, other, best), jnp.where(better, c, split)
    plus = (hop < 4) | ((hop == 4) & (rank < split))
    length = jnp.where(plus, hop, 8 - hop)
    index = jnp.where((hop == 4) & (rank >= split), rank - split, rank)
    twos, threes = jnp.where(plus, n2, n6), jnp.where(plus, n3, n5)
    fours = jnp.where(plus, split, n4 - split)
    odd = twos & 1
    spare = index - threes
    rest = spare - 2 * odd
    lane1 = jnp.where(
        spare < 0,
        fours + index,
        jnp.where(rest < 0, fours + threes + (twos >> 1), fours + threes + ((twos + 1) >> 1) + (rest >> 2)),
    )
    start1 = jnp.where(spare < 0, 3, jnp.where(rest < 0, 2 + spare, rest & 3))
    lane = jnp.where(
        length == 4,
        index,
        jnp.where(length == 3, fours + index, jnp.where(length == 2, fours + threes + (index >> 1), lane1)),
    )
    start = jnp.where(length >= 3, 0, jnp.where(length == 2, 2 * (index & 1), start1))
    first = jnp.where(plus, 0, 32) + 4 * lane + start
    return first, first + length - 1, best


def short_plan(counts, hop, rank):
    m1, m2, m3 = counts
    best, split = jnp.maximum(m1, 2 * m2 + m3), 0 * m2
    for c in range(1, 9):
        other = jnp.maximum(2 * c + m1, 2 * (m2 - c) + m3)
        better = (m2 >= c) & (other < best)
        best, split = jnp.where(better, other, best), jnp.where(better, c, split)
    plus = (hop == 1) | ((hop == 2) & (rank < split))
    index = jnp.where((hop == 2) & (rank >= split), rank - split, rank)
    twos = jnp.where(plus, split, m2 - split)
    lane = jnp.where(hop == 2, index, twos + (index >> 1))
    start = jnp.where(hop == 2, 0, index & 1)
    first = jnp.where(plus, 0, 16) + 2 * lane + start
    return first, first + jnp.where(hop == 2, 1, 0), best


def plan(owner, me):
    square = (32, 32)
    source, target = iota2(square, 0), iota2(square, 1)
    ys, zs, yt, zt = source >> 3, source & 7, target >> 3, target & 7
    along_y, along_z = (yt - ys) & 3, (zt - zs) & 7
    seen = jnp.zeros(square, jnp.int32)
    held, label = [seen, seen], [seen, seen]
    for b in range(24):
        inside = owner[:, b : b + 1] - 24 * target
        match = (inside >= 0) & (inside < 24)
        for p in range(2):
            now = match & (seen == p)
            held[p] = held[p] + jnp.where(now, b, 0)
            label[p] = label[p] + jnp.where(now, inside, 0)
        seen = seen + match.astype(jnp.int32)
    present = seen > 0
    flags = present.astype(jnp.float32)

    def count(first_op, second_op):
        return jnp.dot(first_op, second_op, preferred_element_type=jnp.float32).astype(jnp.int32)

    def mask(condition):
        return condition.astype(jnp.float32)

    same_z, same_y = zs == zt, ys == yt
    rank_az, many_az = count(flags, mask(same_z & (ys < yt))), count(flags, mask(same_z))
    rank_by, many_by = count(flags, mask(same_y & (zs < zt))), count(flags, mask(same_y))
    rank_ay, many_ay = count(mask(same_y & (zt < zs)), flags), count(mask(same_y), flags)
    rank_bz, many_bz = count(mask(same_z & (yt < ys)), flags), count(mask(same_z), flags)
    first_az, last_az, need_az = long_plan([total_of(along_z == k, many_az) for k in range(1, 8)], along_z, rank_az)
    first_bz, last_bz, need_bz = long_plan([total_of(along_z == k, many_bz) for k in range(1, 8)], along_z, rank_bz)
    first_ay, last_ay, need_ay = short_plan([total_of(along_y == k, many_ay) for k in range(1, 4)], along_y, rank_ay)
    first_by, last_by, need_by = short_plan([total_of(along_y == k, many_by) for k in range(1, 4)], along_y, rank_by)

    lanes = iota2((1, 64), 1)
    diagonal = source == target

    def standing(row):
        return jnp.sum(jnp.where(diagonal, row, 0), axis=1, keepdims=True)

    def table(place, values):
        at, value = standing(place), standing(values)
        return jnp.sum(jnp.where(at == lanes, value + 1, 0), axis=0, keepdims=True) - 1

    def own_row(values):
        return jnp.sum(jnp.where(source == me, values, 0), axis=0, keepdims=True)

    my_y, my_z = me >> 3, me & 7
    rows = []
    place = own_row(jnp.where(present & (along_z > 0), first_az, -1))
    rows += [table(place, own_row(held[p])) for p in range(2)]
    place = own_row(jnp.where(present & (along_y > 0), first_by, -1))
    rows += [table(place, own_row(held[p])) for p in range(2)]

    spread_y, spread_z = mask(ys == yt), mask(zs == zt)

    def condense(keep, values, spread, pick):
        moved = count(jnp.where(keep, values, 0).astype(jnp.float32), spread)
        return jnp.sum(jnp.where(pick, moved, 0), axis=0, keepdims=True)

    keep = present & (along_y > 0) & (ys == my_y) & (zt == my_z)
    pick = (ys == my_y) & (zs == zt)
    place = condense(keep, first_ay + 1, spread_y, pick) - 1
    for p in range(2):
        code = jnp.where(along_z == 0, held[p], 32 + last_az)
        rows.append(table(place, condense(keep, code, spread_y, pick)))
    keep = present & (along_z > 0) & (zs == my_z) & (yt == my_y)
    pick = (zs == my_z) & (ys == yt)
    place = condense(keep, first_bz + 1, spread_z, pick) - 1
    for p in range(2):
        code = jnp.where(along_y == 0, held[p], 32 + last_by)
        rows.append(table(place, condense(keep, code, spread_z, pick)))

    def column(values):
        return jnp.sum(jnp.where(target == me, values, 0), axis=1, keepdims=True)

    for first_axis, second_axis, last_one, last_two in ((along_z, along_y, last_az, last_ay), (along_y, along_z, last_by, last_bz)):
        row = jnp.zeros((1, 64), jnp.int32)
        for p in range(2):
            code = jnp.where(
                second_axis > 0,
                160 + 2 * last_two + p,
                jnp.where(first_axis > 0, 32 + 2 * last_one + p, held[p]),
            )
            at, value = column(jnp.where(present, label[p] + 1, 0)) - 1, column(code)
            row = row + jnp.sum(jnp.where(at == lanes, value, 0), axis=0, keepdims=True)
        rows.append(row)
    return rows, jnp.maximum(need_az, need_bz), jnp.maximum(need_ay, need_by)


MESH = pl.DeviceIdType.MESH
BUILDS = ((10, 10), (11, 10), (12, 10), (13, 11), (14, 11), (16, 12), (20, 12), (32, 16))


def along(axis, distance):
    dp = lax.axis_index("dp")
    if axis == "z":
        return ((dp // 8) * 8 + (dp + distance) % 8, lax.axis_index("mp"))
    return ((dp + 8 * distance) % 32, lax.axis_index("mp"))


def meet(devices):
    barrier = pltpu.get_barrier_semaphore()
    for device in devices:
        pl.semaphore_signal(barrier, inc=1, device_id=device, device_id_type=MESH)
    pl.semaphore_wait(barrier, len(devices))


def plan_kernel(slots_ref, table_ref, owner, send_sem, recv_sem):
    dp = lax.axis_index("dp")
    column, row = dp % 8, dp // 8
    ring_z = [along("z", k) for k in range(1, 8)]
    ring_y = [along("y", k) for k in range(1, 4)]
    owner[pl.ds(dp, 1)] = slots_ref[...]
    meet(ring_z + ring_y)
    copies = []
    for k, device in enumerate(ring_z):
        copies.append(
            pltpu.make_async_remote_copy(
                src_ref=owner.at[pl.ds(dp, 1)],
                dst_ref=owner.at[pl.ds(dp, 1)],
                send_sem=send_sem.at[k],
                recv_sem=recv_sem.at[k],
                device_id=device,
                device_id_type=MESH,
            )
        )
        copies[-1].start()
    for copy in copies:
        copy.wait_recv()
    for k, device in enumerate(ring_y):
        copies.append(
            pltpu.make_async_remote_copy(
                src_ref=owner.at[pl.ds(8 * row, 8)],
                dst_ref=owner.at[pl.ds(8 * row, 8)],
                send_sem=send_sem.at[7 + k],
                recv_sem=recv_sem.at[7 + k],
                device_id=device,
                device_id_type=MESH,
            )
        )
        copies[-1].start()
    for copy in copies[7:]:
        copy.wait_recv()
    for copy in copies:
        copy.wait_send()
    rows, need_z, need_y = plan(owner[...].reshape(32, 128), dp)
    for k, entries in enumerate(rows):
        table_ref[k : k + 1, 0:64] = entries
    build = jnp.zeros((1, 1), jnp.int32)
    for steps_z, steps_y in BUILDS[:-1]:
        build = build + jnp.where((need_z > steps_z) | (need_y > steps_y), 1, 0)
    table_ref[10:11, 0:64] = jnp.broadcast_to(build, (1, 64))


def make_plan(owner_slot):
    slots = jnp.pad(owner_slot, (0, 128 - owner_slot.shape[0])).reshape(1, 1, 128)
    return pl.pallas_call(
        plan_kernel,
        out_shape=jax.ShapeDtypeStruct((16, 128), jnp.int32),
        in_specs=[pl.BlockSpec(memory_space=pltpu.VMEM)],
        out_specs=pl.BlockSpec(memory_space=pltpu.VMEM),
        scratch_shapes=[
            pltpu.VMEM((32, 1, 128), jnp.int32),
            pltpu.SemaphoreType.DMA((10,)),
            pltpu.SemaphoreType.DMA((10,)),
        ],
        compiler_params=pltpu.CompilerParams(collective_id=0, has_side_effects=True),
        name="plan",
    )(slots)


class Lanes:
    def __init__(self, axis, steps, rows, columns, table, own, before, sent, got, send_sem, recv_sem):
        self.length, self.half = (4, 32) if axis == "z" else (2, 16)
        self.axis, self.steps, self.rows, self.columns = axis, steps, rows, columns
        self.table, self.own, self.before, self.sent, self.got = table, own, before, sent, got
        self.send_sem, self.recv_sem = send_sem, recv_sem
        self.copies, self.waiting = [], {}

    def value(self, place, p, step):
        code = self.table[self.rows + p, place]
        fresh = self.own[jnp.clip(code, 0, 23), :, self.columns]
        if self.before is not None:
            earlier = self.before[jnp.clip(2 * (code - 32) + p, 0, self.before.shape[0] - 1)]
            fresh = jnp.where(code < 32, fresh, earlier)
        if step == 0:
            return fresh
        return jnp.where(code >= 0, fresh, self.got[2 * (place - 1) + p])

    def step(self, step):
        for lane in range(8):
            if lane * self.length + step >= self.steps:
                continue
            for way in range(2):
                place = way * self.half + lane * self.length + step
                if step > 0:
                    self.waiting.pop((way, lane)).wait_recv()
                for p in range(2):
                    self.sent[2 * place + p] = self.value(place, p, step)
                copy = pltpu.make_async_remote_copy(
                    src_ref=self.sent.at[pl.ds(2 * place, 2)],
                    dst_ref=self.got.at[pl.ds(2 * place, 2)],
                    send_sem=self.send_sem.at[place],
                    recv_sem=self.recv_sem.at[place],
                    device_id=along(self.axis, 1 if way == 0 else -1),
                    device_id_type=MESH,
                )
                copy.start()
                self.copies.append(copy)
                self.waiting[way, lane] = copy

    def arrive(self):
        for copy in self.waiting.values():
            copy.wait_recv()
        self.waiting = {}

    def close(self):
        for copy in self.copies:
            copy.wait_send()


def exchange_kernel(steps_z, steps_y, table, grads, blocks, own, *scratch):
    sent_az, got_az, sent_ay, got_ay, sent_by, got_by, sent_bz, got_bz, pack_a, pack_b = scratch[:10]
    sem_az, sem_ay, sem_by, sem_bz, mp_send, mp_recv, local_sem = scratch[10:]
    mp = lax.axis_index("mp")
    dp = lax.axis_index("dp")
    load = pltpu.make_async_copy(grads, own, local_sem.at[0])
    load.start()
    meet([along("z", 1), along("z", -1), along("y", 1), along("y", -1)] + [(dp, (mp + k) % 8) for k in range(1, 8)])
    load.wait()
    width = own.shape[2] // 2
    left, right = pl.ds(0, width), pl.ds(width, width)
    az = Lanes("z", steps_z, 0, left, table, own, None, sent_az, got_az, sem_az.at[0], sem_az.at[1])
    by = Lanes("y", steps_y, 2, right, table, own, None, sent_by, got_by, sem_by.at[0], sem_by.at[1])
    ay = Lanes("y", steps_y, 4, left, table, own, got_az, sent_ay, got_ay, sem_ay.at[0], sem_ay.at[1])
    bz = Lanes("z", steps_z, 6, right, table, own, got_by, sent_bz, got_bz, sem_bz.at[0], sem_bz.at[1])
    pending = []

    def deliver(row, columns, first, second, pack, number):
        for slot in range(own.shape[0]):
            code = table[row, slot]
            value = jnp.where(
                code < 32,
                own[jnp.clip(code, 0, 23), :, columns],
                jnp.where(
                    code < 160,
                    first[jnp.clip(code - 32, 0, first.shape[0] - 1)],
                    second[jnp.clip(code - 160, 0, second.shape[0] - 1)],
                ),
            )
            pack[slot] = value
        place = blocks.at[:, pl.ds(pl.multiple_of(64 * mp, 64), 64), columns]
        for k in range(1, 8):
            peer = (mp + k) % 8
            copy = pltpu.make_async_remote_copy(
                src_ref=pack.at[pl.ds(3 * peer, 3)],
                dst_ref=place,
                send_sem=mp_send.at[number, k],
                recv_sem=mp_recv.at[number, k],
                device_id=(dp, peer),
                device_id_type=MESH,
            )
            copy.start()
            pending.append(copy)
        copy = pltpu.make_async_copy(pack.at[pl.ds(3 * mp, 3)], place, local_sem.at[1 + number])
        copy.start()
        pending.append(copy)

    for step in range(4):
        az.step(step)
        if step < 2:
            by.step(step)
    by.arrive()
    bz.step(0)
    az.arrive()
    ay.step(0)
    bz.step(1)
    ay.step(1)
    bz.step(2)
    ay.arrive()
    deliver(8, left, got_az, got_ay, pack_a, 0)
    bz.step(3)
    bz.arrive()
    deliver(9, right, got_by, got_bz, pack_b, 1)
    for copy in pending:
        copy.wait()
    for lanes in (az, by, ay, bz):
        lanes.close()


def exchange(number, table, grads):
    steps_z, steps_y = BUILDS[number]
    held, rows, columns = grads.shape
    half = columns // 2
    long, short = pltpu.VMEM((128, rows, half), jnp.bfloat16), pltpu.VMEM((64, rows, half), jnp.bfloat16)
    return pl.pallas_call(
        functools.partial(exchange_kernel, steps_z, steps_y),
        out_shape=jax.ShapeDtypeStruct((3, columns, columns), jnp.bfloat16),
        in_specs=[pl.BlockSpec(memory_space=pltpu.SMEM), pl.BlockSpec(memory_space=pl.ANY)],
        out_specs=pl.BlockSpec(memory_space=pl.ANY),
        scratch_shapes=[
            pltpu.VMEM(grads.shape, jnp.bfloat16),
            long,
            long,
            short,
            short,
            short,
            short,
            long,
            long,
            pltpu.VMEM((held, rows, half), jnp.bfloat16),
            pltpu.VMEM((held, rows, half), jnp.bfloat16),
            pltpu.SemaphoreType.DMA((2, 64)),
            pltpu.SemaphoreType.DMA((2, 32)),
            pltpu.SemaphoreType.DMA((2, 32)),
            pltpu.SemaphoreType.DMA((2, 64)),
            pltpu.SemaphoreType.DMA((2, 8)),
            pltpu.SemaphoreType.DMA((2, 8)),
            pltpu.SemaphoreType.DMA((3,)),
        ],
        compiler_params=pltpu.CompilerParams(
            collective_id=1 + number, has_side_effects=True, vmem_limit_bytes=56 << 20
        ),
        name=f"exchange_{steps_z}_{steps_y}",
    )(table, grads)


def newton_root(matrix):
    size = matrix.shape[0]
    identity = (
        lax.broadcasted_iota(jnp.int32, (size, size), 0) == lax.broadcasted_iota(jnp.int32, (size, size), 1)
    ).astype(jnp.float32)
    wide = matrix.astype(jnp.float32)
    scaling = 2.5 / jnp.sqrt(jnp.sum(wide * wide) + 1e-06)
    scaled = scaling * wide
    squared = (scaling * scaling) * multiply(matrix, matrix)
    shift = (squared - 10.0 * scaled) * 0.0625
    half_shift = shift.astype(jnp.bfloat16)
    quartic = 3.125 * shift + multiply(half_shift, half_shift)
    through = (5.0 * scaled - squared) * 0.25
    fifth = 2.44140625 * through + multiply(quartic.astype(jnp.bfloat16), through.astype(jnp.bfloat16))
    offset = -0.3125 * scaled - 0.25 * fifth
    half_offset = offset.astype(jnp.bfloat16)
    doubled = 3.125 * offset + multiply(half_offset, half_offset)
    half_doubled = doubled.astype(jnp.bfloat16)
    fourth = 4.8828125 * doubled + multiply(half_doubled, half_doubled)
    carried = 1.5625 * scaled + scaling * multiply(half_offset, matrix)
    last = 5.9604644775390625 * carried + multiply(fourth.astype(jnp.bfloat16), carried.astype(jnp.bfloat16))
    root = 1.953125 * identity + 1.25 * offset - 0.25 * last
    return (jnp.sqrt(jnp.sqrt(scaling)) * root).astype(jnp.bfloat16)


def update_kernel(flag_ref, grad_ref, left_ref, right_ref, left_root_ref, right_root_ref, left_out, right_out, dir_out, use_left, use_right):
    slot = pl.program_id(0)
    block = grad_ref[0]
    gram_left = lax.dot_general(block, block, (((1,), (1,)), ((), ())), preferred_element_type=jnp.float32)
    left_out[0] = (decay_rate * left_ref[0].astype(jnp.float32) + (1.0 - decay_rate) * gram_left).astype(jnp.bfloat16)
    gram_right = lax.dot_general(block, block, (((0,), (0,)), ((), ())), preferred_element_type=jnp.float32)
    right_out[0] = (decay_rate * right_ref[0].astype(jnp.float32) + (1.0 - decay_rate) * gram_right).astype(jnp.bfloat16)

    @pl.when(flag_ref[slot] > 0)
    def _():
        use_left[...] = newton_root(left_out[0])
        use_right[...] = newton_root(right_out[0])

    @pl.when(flag_ref[slot] <= 0)
    def _():
        use_left[...] = left_root_ref[0]
        use_right[...] = right_root_ref[0]

    half_way = multiply(use_left[...], block).astype(jnp.bfloat16)
    preconditioned = multiply(half_way, use_right[...])
    wide = block.astype(jnp.float32)
    grad_norm = jnp.sum(wide * wide)
    dir_norm = jnp.sum(preconditioned * preconditioned)
    dir_out[0] = (preconditioned * jnp.sqrt(grad_norm / (dir_norm + 1e-06))).astype(jnp.bfloat16)


def update(refresh_flag, blocks, left_stats, right_stats, left_root, right_root):
    slots, size = blocks.shape[0], blocks.shape[1]
    spec = pl.BlockSpec((1, size, size), lambda k: (k, 0, 0))
    return pl.pallas_call(
        update_kernel,
        grid=(slots,),
        in_specs=[pl.BlockSpec(memory_space=pltpu.SMEM)] + [spec] * 5,
        out_specs=[spec] * 3,
        out_shape=[jax.ShapeDtypeStruct(blocks.shape, jnp.bfloat16)] * 3,
        scratch_shapes=[pltpu.VMEM((size, size), jnp.bfloat16)] * 2,
        compiler_params=pltpu.CompilerParams(vmem_limit_bytes=56 << 20),
        name="update",
    )(refresh_flag, blocks, left_stats, right_stats, left_root, right_root)


def local(grads, owner_slot, refresh_flag, left_stats, right_stats, left_root, right_root):
    table = make_plan(owner_slot)
    builds = [functools.partial(exchange, number) for number in range(len(BUILDS))]
    blocks = lax.switch(table[10, 0], builds, table, grads)
    return tuple(update(refresh_flag, blocks, left_stats, right_stats, left_root, right_root))


def solution(mesh):
    placed = (
        P("dp", "mp", None),
        P("dp"),
        P(("dp", "mp")),
        P(("dp", "mp"), None, None),
        P(("dp", "mp"), None, None),
        P(("dp", "mp"), None, None),
        P(("dp", "mp"), None, None),
    )
    return jax.shard_map(
        local,
        mesh=mesh,
        in_specs=placed,
        out_specs=(
            P(("dp", "mp"), None, None),
            P(("dp", "mp"), None, None),
            P(("dp", "mp"), None, None),
        ),
        check_vma=False,
    )
```

```python
import functools

import jax
import jax.numpy as jnp
from jax import lax
from jax.experimental import pallas as pl
from jax.experimental.pallas import tpu as pltpu
from jax.sharding import PartitionSpec as P

decay_rate = 0.9


def multiply(first_op, second_op):
    return jnp.dot(first_op, second_op, preferred_element_type=jnp.float32)


def iota2(shape, axis):
    return lax.broadcasted_iota(jnp.int32, shape, axis)


def total_of(mask, values):
    return jnp.max(jnp.where(mask, values, 0), keepdims=True)


def long_need(ones, twos, threes, fours):
    odd = twos & 1
    rest = jnp.maximum(ones - threes - 2 * odd, 0)
    lanes = fours + threes + ((twos + 1) >> 1) + ((rest + 3) >> 2)
    spare = ones - threes
    used = jnp.where(
        rest > 0,
        jnp.where((rest & 3) == 0, 4, rest & 3),
        jnp.where(
            twos > 0,
            jnp.where(odd == 1, 2 + jnp.clip(spare, 0, 2), 4),
            jnp.where(threes > 0, jnp.where(spare >= 0, 4, 3), 4),
        ),
    )
    return jnp.where(lanes > 0, 4 * (lanes - 1) + used, 0)


def long_plan(counts, hop, rank):
    n1, n2, n3, n4, n5, n6, n7 = counts
    best, split = long_need(n1, n2, n3, 0 * n4), 0 * n4
    best = jnp.maximum(best, long_need(n7, n6, n5, n4))
    for c in range(1, 5):
        other = jnp.maximum(long_need(n1, n2, n3, 0 * n4 + c), long_need(n7, n6, n5, jnp.maximum(n4 - c, 0)))
        better = (n4 >= c) & (other < best)
        best, split = jnp.where(better, other, best), jnp.where(better, c, split)
    plus = (hop < 4) | ((hop == 4) & (rank < split))
    length = jnp.where(plus, hop, 8 - hop)
    index = jnp.where((hop == 4) & (rank >= split), rank - split, rank)
    twos, threes = jnp.where(plus, n2, n6), jnp.where(plus, n3, n5)
    fours = jnp.where(plus, split, n4 - split)
    odd = twos & 1
    spare = index - threes
    rest = spare - 2 * odd
    lane1 = jnp.where(
        spare < 0,
        fours + index,
        jnp.where(rest < 0, fours + threes + (twos >> 1), fours + threes + ((twos + 1) >> 1) + (rest >> 2)),
    )
    start1 = jnp.where(spare < 0, 3, jnp.where(rest < 0, 2 + spare, rest & 3))
    lane = jnp.where(
        length == 4,
        index,
        jnp.where(length == 3, fours + index, jnp.where(length == 2, fours + threes + (index >> 1), lane1)),
    )
    start = jnp.where(length >= 3, 0, jnp.where(length == 2, 2 * (index & 1), start1))
    first = jnp.where(plus, 0, 32) + 4 * lane + start
    return first, first + length - 1, best


def short_plan(counts, hop, rank):
    m1, m2, m3 = counts
    best, split = jnp.maximum(m1, 2 * m2 + m3), 0 * m2
    for c in range(1, 9):
        other = jnp.maximum(2 * c + m1, 2 * (m2 - c) + m3)
        better = (m2 >= c) & (other < best)
        best, split = jnp.where(better, other, best), jnp.where(better, c, split)
    plus = (hop == 1) | ((hop == 2) & (rank < split))
    index = jnp.where((hop == 2) & (rank >= split), rank - split, rank)
    twos = jnp.where(plus, split, m2 - split)
    lane = jnp.where(hop == 2, index, twos + (index >> 1))
    start = jnp.where(hop == 2, 0, index & 1)
    first = jnp.where(plus, 0, 16) + 2 * lane + start
    return first, first + jnp.where(hop == 2, 1, 0), best


def plan(owner, me):
    square = (32, 32)
    source, target = iota2(square, 0), iota2(square, 1)
    ys, zs, yt, zt = source >> 3, source & 7, target >> 3, target & 7
    along_y, along_z = (yt - ys) & 3, (zt - zs) & 7
    seen = jnp.zeros(square, jnp.int32)
    held, label = [seen, seen], [seen, seen]
    for b in range(24):
        inside = owner[:, b : b + 1] - 24 * target
        match = (inside >= 0) & (inside < 24)
        for p in range(2):
            now = match & (seen == p)
            held[p] = held[p] + jnp.where(now, b, 0)
            label[p] = label[p] + jnp.where(now, inside, 0)
        seen = seen + match.astype(jnp.int32)
    present = seen > 0
    flags = present.astype(jnp.float32)

    def count(first_op, second_op):
        return jnp.dot(first_op, second_op, preferred_element_type=jnp.float32).astype(jnp.int32)

    def mask(condition):
        return condition.astype(jnp.float32)

    same_z, same_y = zs == zt, ys == yt
    rank_az, many_az = count(flags, mask(same_z & (ys < yt))), count(flags, mask(same_z))
    rank_by, many_by = count(flags, mask(same_y & (zs < zt))), count(flags, mask(same_y))
    rank_ay, many_ay = count(mask(same_y & (zt < zs)), flags), count(mask(same_y), flags)
    rank_bz, many_bz = count(mask(same_z & (yt < ys)), flags), count(mask(same_z), flags)
    first_az, last_az, need_az = long_plan([total_of(along_z == k, many_az) for k in range(1, 8)], along_z, rank_az)
    first_bz, last_bz, need_bz = long_plan([total_of(along_z == k, many_bz) for k in range(1, 8)], along_z, rank_bz)
    first_ay, last_ay, need_ay = short_plan([total_of(along_y == k, many_ay) for k in range(1, 4)], along_y, rank_ay)
    first_by, last_by, need_by = short_plan([total_of(along_y == k, many_by) for k in range(1, 4)], along_y, rank_by)

    lanes = iota2((1, 64), 1)
    diagonal = source == target

    def standing(row):
        return jnp.sum(jnp.where(diagonal, row, 0), axis=1, keepdims=True)

    def table(place, values):
        at, value = standing(place), standing(values)
        return jnp.sum(jnp.where(at == lanes, value + 1, 0), axis=0, keepdims=True) - 1

    def own_row(values):
        return jnp.sum(jnp.where(source == me, values, 0), axis=0, keepdims=True)

    my_y, my_z = me >> 3, me & 7
    rows = []
    place = own_row(jnp.where(present & (along_z > 0), first_az, -1))
    rows += [table(place, own_row(held[p])) for p in range(2)]
    place = own_row(jnp.where(present & (along_y > 0), first_by, -1))
    rows += [table(place, own_row(held[p])) for p in range(2)]

    spread_y, spread_z = mask(ys == yt), mask(zs == zt)

    def condense(keep, values, spread, pick):
        moved = count(jnp.where(keep, values, 0).astype(jnp.float32), spread)
        return jnp.sum(jnp.where(pick, moved, 0), axis=0, keepdims=True)

    keep = present & (along_y > 0) & (ys == my_y) & (zt == my_z)
    pick = (ys == my_y) & (zs == zt)
    place = condense(keep, first_ay + 1, spread_y, pick) - 1
    for p in range(2):
        code = jnp.where(along_z == 0, held[p], 32 + last_az)
        rows.append(table(place, condense(keep, code, spread_y, pick)))
    keep = present & (along_z > 0) & (zs == my_z) & (yt == my_y)
    pick = (zs == my_z) & (ys == yt)
    place = condense(keep, first_bz + 1, spread_z, pick) - 1
    for p in range(2):
        code = jnp.where(along_y == 0, held[p], 32 + last_by)
        rows.append(table(place, condense(keep, code, spread_z, pick)))

    def column(values):
        return jnp.sum(jnp.where(target == me, values, 0), axis=1, keepdims=True)

    for first_axis, second_axis, last_one, last_two in ((along_z, along_y, last_az, last_ay), (along_y, along_z, last_by, last_bz)):
        row = jnp.zeros((1, 64), jnp.int32)
        for p in range(2):
            code = jnp.where(
                second_axis > 0,
                160 + 2 * last_two + p,
                jnp.where(first_axis > 0, 32 + 2 * last_one + p, held[p]),
            )
            at, value = column(jnp.where(present, label[p] + 1, 0)) - 1, column(code)
            row = row + jnp.sum(jnp.where(at == lanes, value, 0), axis=0, keepdims=True)
        rows.append(row)
    return rows, jnp.maximum(need_az, need_bz), jnp.maximum(need_ay, need_by)


MESH = pl.DeviceIdType.MESH
BUILDS = ((10, 10), (11, 10), (12, 10), (13, 11), (14, 11), (16, 12), (20, 12), (32, 16))


def along(axis, distance):
    dp = lax.axis_index("dp")
    if axis == "z":
        return ((dp // 8) * 8 + (dp + distance) % 8, lax.axis_index("mp"))
    return ((dp + 8 * distance) % 32, lax.axis_index("mp"))


def meet(devices):
    barrier = pltpu.get_barrier_semaphore()
    for device in devices:
        pl.semaphore_signal(barrier, inc=1, device_id=device, device_id_type=MESH)
    pl.semaphore_wait(barrier, len(devices))


def plan_kernel(slots_ref, table_ref, owner, send_sem, recv_sem):
    dp = lax.axis_index("dp")
    column, row = dp % 8, dp // 8
    ring_z = [along("z", k) for k in range(1, 8)]
    ring_y = [along("y", k) for k in range(1, 4)]
    owner[pl.ds(dp, 1)] = slots_ref[...]
    meet(ring_z + ring_y)
    copies = []
    for k, device in enumerate(ring_z):
        copies.append(
            pltpu.make_async_remote_copy(
                src_ref=owner.at[pl.ds(dp, 1)],
                dst_ref=owner.at[pl.ds(dp, 1)],
                send_sem=send_sem.at[k],
                recv_sem=recv_sem.at[k],
                device_id=device,
                device_id_type=MESH,
            )
        )
        copies[-1].start()
    for copy in copies:
        copy.wait_recv()
    for k, device in enumerate(ring_y):
        copies.append(
            pltpu.make_async_remote_copy(
                src_ref=owner.at[pl.ds(8 * row, 8)],
                dst_ref=owner.at[pl.ds(8 * row, 8)],
                send_sem=send_sem.at[7 + k],
                recv_sem=recv_sem.at[7 + k],
                device_id=device,
                device_id_type=MESH,
            )
        )
        copies[-1].start()
    for copy in copies[7:]:
        copy.wait_recv()
    for copy in copies:
        copy.wait_send()
    rows, need_z, need_y = plan(owner[...].reshape(32, 128), dp)
    for k, entries in enumerate(rows):
        table_ref[k : k + 1, 0:64] = entries
    build = jnp.zeros((1, 1), jnp.int32)
    for steps_z, steps_y in BUILDS[:-1]:
        build = build + jnp.where((need_z > steps_z) | (need_y > steps_y), 1, 0)
    table_ref[10:11, 0:64] = jnp.broadcast_to(build, (1, 64))


def make_plan(owner_slot):
    slots = jnp.pad(owner_slot, (0, 128 - owner_slot.shape[0])).reshape(1, 1, 128)
    return pl.pallas_call(
        plan_kernel,
        out_shape=jax.ShapeDtypeStruct((16, 128), jnp.int32),
        in_specs=[pl.BlockSpec(memory_space=pltpu.VMEM)],
        out_specs=pl.BlockSpec(memory_space=pltpu.VMEM),
        scratch_shapes=[
            pltpu.VMEM((32, 1, 128), jnp.int32),
            pltpu.SemaphoreType.DMA((10,)),
            pltpu.SemaphoreType.DMA((10,)),
        ],
        compiler_params=pltpu.CompilerParams(collective_id=0, has_side_effects=True),
        name="plan",
    )(slots)


class Lanes:
    def __init__(self, axis, steps, rows, columns, table, own, before, sent, got, send_sem, recv_sem):
        self.length, self.half = (4, 32) if axis == "z" else (2, 16)
        self.axis, self.steps, self.rows, self.columns = axis, steps, rows, columns
        self.table, self.own, self.before, self.sent, self.got = table, own, before, sent, got
        self.send_sem, self.recv_sem = send_sem, recv_sem

    def value(self, place, p, step):
        code = self.table[self.rows + p, place]
        fresh = self.own[jnp.clip(code, 0, 23), :, self.columns]
        if self.before is not None:
            earlier = self.before[jnp.clip(2 * (code - 32) + p, 0, self.before.shape[0] - 1)]
            fresh = jnp.where(code < 32, fresh, earlier)
        if step == 0:
            return fresh
        return jnp.where(code >= 0, fresh, self.got[2 * (place - 1) + p])

    def copy(self, place, way):
        return pltpu.make_async_remote_copy(
            src_ref=self.sent.at[pl.ds(2 * place, 2)],
            dst_ref=self.got.at[pl.ds(2 * place, 2)],
            send_sem=self.send_sem.at[place],
            recv_sem=self.recv_sem.at[place],
            device_id=along(self.axis, 1 - 2 * way),
            device_id_type=MESH,
        )

    def each(self, step, action):
        lanes = (self.steps - step + self.length - 1) // self.length

        def body(lane, carry):
            for way in range(2):
                action(way * self.half + lane * self.length + step, way)
            return carry

        lax.fori_loop(0, lanes, body, 0)

    def step(self, step):
        def action(place, way):
            if step > 0:
                self.copy(place - 1, way).wait_recv()
            for p in range(2):
                self.sent[2 * place + p] = self.value(place, p, step)
            self.copy(place, way).start()

        self.each(step, action)

    def arrive(self):
        def body(lane, carry):
            for way in range(2):
                self.copy(way * self.half + lane * self.length + self.length - 1, way).wait_recv()
            return carry

        whole, part = self.steps // self.length, self.steps % self.length
        lax.fori_loop(0, whole, body, 0)
        if part:
            for way in range(2):
                self.copy(way * self.half + whole * self.length + part - 1, way).wait_recv()

    def close(self):
        for step in range(self.length):
            self.each(step, lambda place, way: self.copy(place, way).wait_send())


def exchange_kernel(steps_z, steps_y, table, grads, blocks, own, *scratch):
    sent_az, got_az, sent_ay, got_ay, sent_by, got_by, sent_bz, got_bz, pack_a, pack_b = scratch[:10]
    sem_az, sem_ay, sem_by, sem_bz, mp_send, mp_recv, local_sem = scratch[10:]
    mp = lax.axis_index("mp")
    dp = lax.axis_index("dp")
    load = pltpu.make_async_copy(grads, own, local_sem.at[0])
    load.start()
    meet([along("z", 1), along("z", -1), along("y", 1), along("y", -1)] + [(dp, (mp + k) % 8) for k in range(1, 8)])
    load.wait()
    width = own.shape[2] // 2
    left, right = pl.ds(0, width), pl.ds(width, width)
    az = Lanes("z", steps_z, 0, left, table, own, None, sent_az, got_az, sem_az.at[0], sem_az.at[1])
    by = Lanes("y", steps_y, 2, right, table, own, None, sent_by, got_by, sem_by.at[0], sem_by.at[1])
    ay = Lanes("y", steps_y, 4, left, table, own, got_az, sent_ay, got_ay, sem_ay.at[0], sem_ay.at[1])
    bz = Lanes("z", steps_z, 6, right, table, own, got_by, sent_bz, got_bz, sem_bz.at[0], sem_bz.at[1])
    pending = []

    def deliver(row, columns, first, second, pack, number):
        def body(slot, carry):
            code = table[row, slot]
            pack[slot] = jnp.where(
                code < 32,
                own[jnp.clip(code, 0, 23), :, columns],
                jnp.where(
                    code < 160,
                    first[jnp.clip(code - 32, 0, first.shape[0] - 1)],
                    second[jnp.clip(code - 160, 0, second.shape[0] - 1)],
                ),
            )
            return carry

        lax.fori_loop(0, own.shape[0], body, 0)
        place = blocks.at[:, pl.ds(pl.multiple_of(64 * mp, 64), 64), columns]
        for k in range(1, 8):
            peer = (mp + k) % 8
            copy = pltpu.make_async_remote_copy(
                src_ref=pack.at[pl.ds(3 * peer, 3)],
                dst_ref=place,
                send_sem=mp_send.at[number, k],
                recv_sem=mp_recv.at[number, k],
                device_id=(dp, peer),
                device_id_type=MESH,
            )
            copy.start()
            pending.append(copy)
        copy = pltpu.make_async_copy(pack.at[pl.ds(3 * mp, 3)], place, local_sem.at[1 + number])
        copy.start()
        pending.append(copy)

    for step in range(4):
        az.step(step)
        if step < 2:
            by.step(step)
    by.arrive()
    bz.step(0)
    az.arrive()
    ay.step(0)
    bz.step(1)
    ay.step(1)
    bz.step(2)
    ay.arrive()
    deliver(8, left, got_az, got_ay, pack_a, 0)
    bz.step(3)
    bz.arrive()
    deliver(9, right, got_by, got_bz, pack_b, 1)
    for copy in pending:
        copy.wait()
    for lanes in (az, by, ay, bz):
        lanes.close()


def exchange(number, table, grads):
    steps_z, steps_y = BUILDS[number]
    held, rows, columns = grads.shape
    half = columns // 2
    long, short = pltpu.VMEM((128, rows, half), jnp.bfloat16), pltpu.VMEM((64, rows, half), jnp.bfloat16)
    return pl.pallas_call(
        functools.partial(exchange_kernel, steps_z, steps_y),
        out_shape=jax.ShapeDtypeStruct((3, columns, columns), jnp.bfloat16),
        in_specs=[pl.BlockSpec(memory_space=pltpu.SMEM), pl.BlockSpec(memory_space=pl.ANY)],
        out_specs=pl.BlockSpec(memory_space=pl.ANY),
        scratch_shapes=[
            pltpu.VMEM(grads.shape, jnp.bfloat16),
            long,
            long,
            short,
            short,
            short,
            short,
            long,
            long,
            pltpu.VMEM((held, rows, half), jnp.bfloat16),
            pltpu.VMEM((held, rows, half), jnp.bfloat16),
            pltpu.SemaphoreType.DMA((2, 64)),
            pltpu.SemaphoreType.DMA((2, 32)),
            pltpu.SemaphoreType.DMA((2, 32)),
            pltpu.SemaphoreType.DMA((2, 64)),
            pltpu.SemaphoreType.DMA((2, 8)),
            pltpu.SemaphoreType.DMA((2, 8)),
            pltpu.SemaphoreType.DMA((3,)),
        ],
        compiler_params=pltpu.CompilerParams(
            collective_id=1 + number, has_side_effects=True, vmem_limit_bytes=56 << 20
        ),
        name=f"exchange_{steps_z}_{steps_y}",
    )(table, grads)


def newton_root(matrix):
    size = matrix.shape[0]
    identity = (
        lax.broadcasted_iota(jnp.int32, (size, size), 0) == lax.broadcasted_iota(jnp.int32, (size, size), 1)
    ).astype(jnp.float32)
    wide = matrix.astype(jnp.float32)
    scaling = 2.5 / jnp.sqrt(jnp.sum(wide * wide) + 1e-06)
    scaled = scaling * wide
    squared = (scaling * scaling) * multiply(matrix, matrix)
    shift = (squared - 10.0 * scaled) * 0.0625
    half_shift = shift.astype(jnp.bfloat16)
    quartic = 3.125 * shift + multiply(half_shift, half_shift)
    through = (5.0 * scaled - squared) * 0.25
    fifth = 2.44140625 * through + multiply(quartic.astype(jnp.bfloat16), through.astype(jnp.bfloat16))
    offset = -0.3125 * scaled - 0.25 * fifth
    half_offset = offset.astype(jnp.bfloat16)
    doubled = 3.125 * offset + multiply(half_offset, half_offset)
    half_doubled = doubled.astype(jnp.bfloat16)
    fourth = 4.8828125 * doubled + multiply(half_doubled, half_doubled)
    carried = 1.5625 * scaled + scaling * multiply(half_offset, matrix)
    last = 5.9604644775390625 * carried + multiply(fourth.astype(jnp.bfloat16), carried.astype(jnp.bfloat16))
    root = 1.953125 * identity + 1.25 * offset - 0.25 * last
    return (jnp.sqrt(jnp.sqrt(scaling)) * root).astype(jnp.bfloat16)


def update_kernel(flag_ref, grad_ref, left_ref, right_ref, left_root_ref, right_root_ref, left_out, right_out, dir_out, use_left, use_right):
    slot = pl.program_id(0)
    block = grad_ref[0]
    gram_left = lax.dot_general(block, block, (((1,), (1,)), ((), ())), preferred_element_type=jnp.float32)
    left_out[0] = (decay_rate * left_ref[0].astype(jnp.float32) + (1.0 - decay_rate) * gram_left).astype(jnp.bfloat16)
    gram_right = lax.dot_general(block, block, (((0,), (0,)), ((), ())), preferred_element_type=jnp.float32)
    right_out[0] = (decay_rate * right_ref[0].astype(jnp.float32) + (1.0 - decay_rate) * gram_right).astype(jnp.bfloat16)

    @pl.when(flag_ref[slot] > 0)
    def _():
        use_left[...] = newton_root(left_out[0])
        use_right[...] = newton_root(right_out[0])

    @pl.when(flag_ref[slot] <= 0)
    def _():
        use_left[...] = left_root_ref[0]
        use_right[...] = right_root_ref[0]

    half_way = multiply(use_left[...], block).astype(jnp.bfloat16)
    preconditioned = multiply(half_way, use_right[...])
    wide = block.astype(jnp.float32)
    grad_norm = jnp.sum(wide * wide)
    dir_norm = jnp.sum(preconditioned * preconditioned)
    dir_out[0] = (preconditioned * jnp.sqrt(grad_norm / (dir_norm + 1e-06))).astype(jnp.bfloat16)


def update(refresh_flag, blocks, left_stats, right_stats, left_root, right_root):
    slots, size = blocks.shape[0], blocks.shape[1]
    spec = pl.BlockSpec((1, size, size), lambda k: (k, 0, 0))
    return pl.pallas_call(
        update_kernel,
        grid=(slots,),
        in_specs=[pl.BlockSpec(memory_space=pltpu.SMEM)] + [spec] * 5,
        out_specs=[spec] * 3,
        out_shape=[jax.ShapeDtypeStruct(blocks.shape, jnp.bfloat16)] * 3,
        scratch_shapes=[pltpu.VMEM((size, size), jnp.bfloat16)] * 2,
        compiler_params=pltpu.CompilerParams(vmem_limit_bytes=56 << 20),
        name="update",
    )(refresh_flag, blocks, left_stats, right_stats, left_root, right_root)


def local(grads, owner_slot, refresh_flag, left_stats, right_stats, left_root, right_root):
    table = make_plan(owner_slot)
    builds = [functools.partial(exchange, number) for number in range(len(BUILDS))]
    blocks = lax.switch(table[10, 0], builds, table, grads)
    return tuple(update(refresh_flag, blocks, left_stats, right_stats, left_root, right_root))


def solution(mesh):
    placed = (
        P("dp", "mp", None),
        P("dp"),
        P(("dp", "mp")),
        P(("dp", "mp"), None, None),
        P(("dp", "mp"), None, None),
        P(("dp", "mp"), None, None),
        P(("dp", "mp"), None, None),
    )
    return jax.shard_map(
        local,
        mesh=mesh,
        in_specs=placed,
        out_specs=(
            P(("dp", "mp"), None, None),
            P(("dp", "mp"), None, None),
            P(("dp", "mp"), None, None),
        ),
        check_vma=False,
    )
```

```python
import functools

import jax
import jax.numpy as jnp
from jax import lax
from jax.experimental import pallas as pl
from jax.experimental.pallas import tpu as pltpu
from jax.sharding import PartitionSpec as P

decay_rate = 0.9


def multiply(first_op, second_op):
    return jnp.dot(first_op, second_op, preferred_element_type=jnp.float32)


def iota2(shape, axis):
    return lax.broadcasted_iota(jnp.int32, shape, axis)


def total_of(mask, values):
    return jnp.max(jnp.where(mask, values, 0), keepdims=True)


def long_need(ones, twos, threes, fours):
    odd = twos & 1
    rest = jnp.maximum(ones - threes - 2 * odd, 0)
    lanes = fours + threes + ((twos + 1) >> 1) + ((rest + 3) >> 2)
    spare = ones - threes
    used = jnp.where(
        rest > 0,
        jnp.where((rest & 3) == 0, 4, rest & 3),
        jnp.where(
            twos > 0,
            jnp.where(odd == 1, 2 + jnp.clip(spare, 0, 2), 4),
            jnp.where(threes > 0, jnp.where(spare >= 0, 4, 3), 4),
        ),
    )
    return jnp.where(lanes > 0, 4 * (lanes - 1) + used, 0)


def long_plan(counts, hop, rank):
    n1, n2, n3, n4, n5, n6, n7 = counts
    best, split = long_need(n1, n2, n3, 0 * n4), 0 * n4
    best = jnp.maximum(best, long_need(n7, n6, n5, n4))
    for c in range(1, 5):
        other = jnp.maximum(long_need(n1, n2, n3, 0 * n4 + c), long_need(n7, n6, n5, jnp.maximum(n4 - c, 0)))
        better = (n4 >= c) & (other < best)
        best, split = jnp.where(better, other, best), jnp.where(better, c, split)
    plus = (hop < 4) | ((hop == 4) & (rank < split))
    length = jnp.where(plus, hop, 8 - hop)
    index = jnp.where((hop == 4) & (rank >= split), rank - split, rank)
    twos, threes = jnp.where(plus, n2, n6), jnp.where(plus, n3, n5)
    fours = jnp.where(plus, split, n4 - split)
    odd = twos & 1
    spare = index - threes
    rest = spare - 2 * odd
    lane1 = jnp.where(
        spare < 0,
        fours + index,
        jnp.where(rest < 0, fours + threes + (twos >> 1), fours + threes + ((twos + 1) >> 1) + (rest >> 2)),
    )
    start1 = jnp.where(spare < 0, 3, jnp.where(rest < 0, 2 + spare, rest & 3))
    lane = jnp.where(
        length == 4,
        index,
        jnp.where(length == 3, fours + index, jnp.where(length == 2, fours + threes + (index >> 1), lane1)),
    )
    start = jnp.where(length >= 3, 0, jnp.where(length == 2, 2 * (index & 1), start1))
    first = jnp.where(plus, 0, 32) + 4 * lane + start
    return first, first + length - 1, best


def short_plan(counts, hop, rank):
    m1, m2, m3 = counts
    best, split = jnp.maximum(m1, 2 * m2 + m3), 0 * m2
    for c in range(1, 9):
        other = jnp.maximum(2 * c + m1, 2 * (m2 - c) + m3)
        better = (m2 >= c) & (other < best)
        best, split = jnp.where(better, other, best), jnp.where(better, c, split)
    plus = (hop == 1) | ((hop == 2) & (rank < split))
    index = jnp.where((hop == 2) & (rank >= split), rank - split, rank)
    twos = jnp.where(plus, split, m2 - split)
    lane = jnp.where(hop == 2, index, twos + (index >> 1))
    start = jnp.where(hop == 2, 0, index & 1)
    first = jnp.where(plus, 0, 16) + 2 * lane + start
    return first, first + jnp.where(hop == 2, 1, 0), best


def plan(owner, me):
    square = (32, 32)
    source, target = iota2(square, 0), iota2(square, 1)
    ys, zs, yt, zt = source >> 3, source & 7, target >> 3, target & 7
    along_y, along_z = (yt - ys) & 3, (zt - zs) & 7
    seen = jnp.zeros(square, jnp.int32)
    held, label = [seen, seen], [seen, seen]
    for b in range(24):
        inside = owner[:, b : b + 1] - 24 * target
        match = (inside >= 0) & (inside < 24)
        for p in range(2):
            now = match & (seen == p)
            held[p] = held[p] + jnp.where(now, b, 0)
            label[p] = label[p] + jnp.where(now, inside, 0)
        seen = seen + match.astype(jnp.int32)
    present = seen > 0
    flags = present.astype(jnp.float32)

    def count(first_op, second_op):
        return jnp.dot(first_op, second_op, preferred_element_type=jnp.float32).astype(jnp.int32)

    def mask(condition):
        return condition.astype(jnp.float32)

    same_z, same_y = zs == zt, ys == yt
    rank_az, many_az = count(flags, mask(same_z & (ys < yt))), count(flags, mask(same_z))
    rank_by, many_by = count(flags, mask(same_y & (zs < zt))), count(flags, mask(same_y))
    rank_ay, many_ay = count(mask(same_y & (zt < zs)), flags), count(mask(same_y), flags)
    rank_bz, many_bz = count(mask(same_z & (yt < ys)), flags), count(mask(same_z), flags)
    first_az, last_az, need_az = long_plan([total_of(along_z == k, many_az) for k in range(1, 8)], along_z, rank_az)
    first_bz, last_bz, need_bz = long_plan([total_of(along_z == k, many_bz) for k in range(1, 8)], along_z, rank_bz)
    first_ay, last_ay, need_ay = short_plan([total_of(along_y == k, many_ay) for k in range(1, 4)], along_y, rank_ay)
    first_by, last_by, need_by = short_plan([total_of(along_y == k, many_by) for k in range(1, 4)], along_y, rank_by)

    lanes = iota2((1, 64), 1)
    diagonal = source == target

    def standing(row):
        return jnp.sum(jnp.where(diagonal, row, 0), axis=1, keepdims=True)

    def table(place, values):
        at, value = standing(place), standing(values)
        return jnp.sum(jnp.where(at == lanes, value + 1, 0), axis=0, keepdims=True) - 1

    def own_row(values):
        return jnp.sum(jnp.where(source == me, values, 0), axis=0, keepdims=True)

    my_y, my_z = me >> 3, me & 7
    rows = []
    place = own_row(jnp.where(present & (along_z > 0), first_az, -1))
    rows += [table(place, own_row(held[p])) for p in range(2)]
    place = own_row(jnp.where(present & (along_y > 0), first_by, -1))
    rows += [table(place, own_row(held[p])) for p in range(2)]

    spread_y, spread_z = mask(ys == yt), mask(zs == zt)

    def condense(keep, values, spread, pick):
        moved = count(jnp.where(keep, values, 0).astype(jnp.float32), spread)
        return jnp.sum(jnp.where(pick, moved, 0), axis=0, keepdims=True)

    keep = present & (along_y > 0) & (ys == my_y) & (zt == my_z)
    pick = (ys == my_y) & (zs == zt)
    place = condense(keep, first_ay + 1, spread_y, pick) - 1
    for p in range(2):
        code = jnp.where(along_z == 0, held[p], 32 + last_az)
        rows.append(table(place, condense(keep, code, spread_y, pick)))
    keep = present & (along_z > 0) & (zs == my_z) & (yt == my_y)
    pick = (zs == my_z) & (ys == yt)
    place = condense(keep, first_bz + 1, spread_z, pick) - 1
    for p in range(2):
        code = jnp.where(along_y == 0, held[p], 32 + last_by)
        rows.append(table(place, condense(keep, code, spread_z, pick)))

    def column(values):
        return jnp.sum(jnp.where(target == me, values, 0), axis=1, keepdims=True)

    for first_axis, second_axis, last_one, last_two in ((along_z, along_y, last_az, last_ay), (along_y, along_z, last_by, last_bz)):
        row = jnp.zeros((1, 64), jnp.int32)
        for p in range(2):
            code = jnp.where(
                second_axis > 0,
                160 + 2 * last_two + p,
                jnp.where(first_axis > 0, 32 + 2 * last_one + p, held[p]),
            )
            at, value = column(jnp.where(present, label[p] + 1, 0)) - 1, column(code)
            row = row + jnp.sum(jnp.where(at == lanes, value, 0), axis=0, keepdims=True)
        rows.append(row)
    return rows, jnp.maximum(need_az, need_bz), jnp.maximum(need_ay, need_by)


MESH = pl.DeviceIdType.MESH
BUILDS = ((10, 9), (12, 8), (12, 9), (14, 9), (14, 11), (16, 10), (20, 12), (32, 16))


def along(axis, distance):
    dp = lax.axis_index("dp")
    if axis == "z":
        return ((dp // 8) * 8 + (dp + distance) % 8, lax.axis_index("mp"))
    return ((dp + 8 * distance) % 32, lax.axis_index("mp"))


def meet(devices):
    barrier = pltpu.get_barrier_semaphore()
    for device in devices:
        pl.semaphore_signal(barrier, inc=1, device_id=device, device_id_type=MESH)
    pl.semaphore_wait(barrier, len(devices))


def plan_kernel(slots_ref, table_ref, build_ref, owner, send_sem, recv_sem):
    dp = lax.axis_index("dp")
    row = dp // 8
    ring_z = [along("z", k) for k in range(1, 8)]
    ring_y = [along("y", k) for k in range(1, 4)]
    owner[pl.ds(dp, 1)] = slots_ref[...]
    meet(ring_z + ring_y)
    copies = []
    for k, device in enumerate(ring_z):
        copies.append(
            pltpu.make_async_remote_copy(
                src_ref=owner.at[pl.ds(dp, 1)],
                dst_ref=owner.at[pl.ds(dp, 1)],
                send_sem=send_sem.at[k],
                recv_sem=recv_sem.at[k],
                device_id=device,
                device_id_type=MESH,
            )
        )
        copies[-1].start()
    for copy in copies:
        copy.wait_recv()
    for k, device in enumerate(ring_y):
        copies.append(
            pltpu.make_async_remote_copy(
                src_ref=owner.at[pl.ds(8 * row, 8)],
                dst_ref=owner.at[pl.ds(8 * row, 8)],
                send_sem=send_sem.at[7 + k],
                recv_sem=recv_sem.at[7 + k],
                device_id=device,
                device_id_type=MESH,
            )
        )
        copies[-1].start()
    for copy in copies[7:]:
        copy.wait_recv()
    for copy in copies:
        copy.wait_send()
    rows, need_z, need_y = plan(owner[...].reshape(32, 128), dp)
    for k, entries in enumerate(rows):
        table_ref[k : k + 1, 0:64] = entries
    build = jnp.full((1, 1), len(BUILDS) - 1, jnp.int32)
    for number in range(len(BUILDS) - 2, -1, -1):
        steps_z, steps_y = BUILDS[number]
        build = jnp.where((need_z <= steps_z) & (need_y <= steps_y), number, build)
    build_ref[...] = build


def make_plan(owner_slot):
    slots = jnp.pad(owner_slot, (0, 128 - owner_slot.shape[0])).reshape(1, 1, 128)
    vmem = pl.BlockSpec(memory_space=pltpu.VMEM)
    return pl.pallas_call(
        plan_kernel,
        out_shape=[jax.ShapeDtypeStruct((16, 128), jnp.int32), jax.ShapeDtypeStruct((1, 1), jnp.int32)],
        in_specs=[vmem],
        out_specs=[vmem, vmem],
        scratch_shapes=[
            pltpu.VMEM((32, 1, 128), jnp.int32),
            pltpu.SemaphoreType.DMA((10,)),
            pltpu.SemaphoreType.DMA((10,)),
        ],
        compiler_params=pltpu.CompilerParams(collective_id=0, has_side_effects=True),
        name="plan",
    )(slots)


class Lanes:
    def __init__(self, near, steps, rows, columns, table, own, before, buffers, sems):
        self.near, self.length, self.half = near
        self.steps, self.rows, self.columns = steps, rows, columns
        self.table, self.own, self.before = table, own, before
        self.sent, self.got = buffers
        self.send_sem, self.recv_sem = sems

    def received(self, entry, columns):
        unused = jnp.where(entry >= 2 * self.half, 2 * (self.half - self.steps), 0)
        return self.got[jnp.clip(entry - unused, 0, 4 * self.steps - 1), :, columns]

    def value(self, way, at, p, step):
        code = self.table[self.rows + p, way * self.half + at]
        fresh = self.own[jnp.clip(code, 0, 23), :, self.columns]
        if self.before is not None:
            lanes, columns = self.before
            fresh = jnp.where(code < 32, fresh, lanes.received(2 * (code - 32) + p, columns))
        if step == 0:
            return fresh
        return jnp.where(code >= 0, fresh, self.got[2 * (way * self.steps + at - 1) + p])

    def copy(self, way, at):
        plus, minus = self.near
        place = way * self.steps + at
        return pltpu.make_async_remote_copy(
            src_ref=self.sent.at[pl.ds(2 * place, 2)],
            dst_ref=self.got.at[pl.ds(2 * place, 2)],
            send_sem=self.send_sem.at[0],
            recv_sem=self.recv_sem.at[place],
            device_id=(plus + way * (minus - plus), lax.axis_index("mp")),
            device_id_type=MESH,
        )

    def each(self, step, action):
        lanes = (self.steps - step + self.length - 1) // self.length

        def body(number, carry):
            action(number % 2, number // 2 * self.length + step)
            return carry

        lax.fori_loop(0, 2 * lanes, body, 0)

    def fill(self, way, at, step):
        for p in range(2):
            self.sent[2 * (way * self.steps + at) + p] = self.value(way, at, p, step)

    def ready(self):
        self.each(0, lambda way, at: self.fill(way, at, 0))

    def leave(self):
        self.each(0, lambda way, at: self.copy(way, at).start())

    def step(self, step):
        def action(way, at):
            if step > 0:
                self.copy(way, at - 1).wait_recv()
            self.fill(way, at, step)
            self.copy(way, at).start()

        self.each(step, action)

    def arrive(self):
        whole, part = self.steps // self.length, self.steps % self.length

        def body(number, carry):
            lane = number // 2
            last = jnp.where(lane < whole, self.length, part) - 1
            self.copy(number % 2, lane * self.length + last).wait_recv()
            return carry

        lax.fori_loop(0, 2 * (whole + (part > 0)), body, 0)

    def close(self):
        pltpu.make_async_remote_copy(
            src_ref=self.sent,
            dst_ref=self.got,
            send_sem=self.send_sem.at[0],
            recv_sem=self.recv_sem.at[0],
            device_id=(self.near[0], lax.axis_index("mp")),
            device_id_type=MESH,
        ).wait_send()


def exchange_kernel(steps_z, steps_y, table, grads, blocks, own, *scratch):
    buffers_by = scratch[0:2]
    buffers_az, buffers_ay, buffers_bz = ((scratch[k : k + 2], scratch[k + 2 : k + 4]) for k in (2, 6, 10))
    packs = scratch[14]
    sems = [(scratch[15 + 2 * k], scratch[16 + 2 * k]) for k in range(7)]
    mp_send, mp_recv, local_sem = scratch[29:]
    mp = lax.axis_index("mp")
    dp = lax.axis_index("dp")
    load = pltpu.make_async_copy(grads, own, local_sem.at[4])
    load.start()
    barrier = pltpu.get_barrier_semaphore()
    row = (dp // 8) * 8
    near_z = (row + (dp + 1) % 8, row + (dp + 7) % 8)
    near_y = ((dp + 8) % 32, (dp + 24) % 32)
    for device in near_z + near_y:
        pl.semaphore_signal(barrier, inc=1, device_id=(device, mp), device_id_type=MESH)

    def greet(k, carry):
        pl.semaphore_signal(barrier, inc=1, device_id=(dp, (mp + k) % 8), device_id_type=MESH)
        return carry

    lax.fori_loop(1, 8, greet, 0)
    half = own.shape[2] // 2
    quarter = half // 2
    quarters = [pl.ds(k * quarter, quarter) for k in range(4)]
    by = Lanes((near_y, 2, 16), steps_y, 2, pl.ds(half, half), table, own, None, buffers_by, sems[0])
    az1, az2 = (
        Lanes((near_z, 4, 32), steps_z, 0, quarters[k], table, own, None, buffers_az[k], sems[1 + k])
        for k in range(2)
    )
    ay1, ay2 = (
        Lanes((near_y, 2, 16), steps_y, 4, quarters[k], table, own, ((az1, az2)[k], quarters[0]), buffers_ay[k], sems[3 + k])
        for k in range(2)
    )
    bz1, bz2 = (
        Lanes((near_z, 4, 32), steps_z, 6, quarters[2 + k], table, own, (by, quarters[k]), buffers_bz[k], sems[5 + k])
        for k in range(2)
    )
    load.wait()
    az1.ready()
    pl.semaphore_wait(barrier, 11)

    def place(number):
        return blocks.at[:, pl.ds(pl.multiple_of(64 * mp, 64), 64), quarters[number]]

    def spread(number, k):
        peer = (mp + k) % 8
        return pltpu.make_async_remote_copy(
            src_ref=packs.at[number, pl.ds(3 * peer, 3)],
            dst_ref=place(number),
            send_sem=mp_send.at[number],
            recv_sem=mp_recv.at[number, k],
            device_id=(dp, peer),
            device_id_type=MESH,
        )

    def keep(number):
        return pltpu.make_async_copy(packs.at[number, pl.ds(3 * mp, 3)], place(number), local_sem.at[number])

    def deliver(row, number, lanes):
        columns = quarters[number]
        first, first_columns = lanes.before

        def body(slot, carry):
            code = table[row, slot]
            packs[number, slot] = jnp.where(
                code < 32,
                own[jnp.clip(code, 0, 23), :, columns],
                jnp.where(
                    code < 160,
                    first.received(code - 32, first_columns),
                    lanes.received(code - 160, quarters[0]),
                ),
            )
            return carry

        lax.fori_loop(0, own.shape[0], body, 0)
        def send(k, carry):
            spread(number, k).start()
            return carry

        lax.fori_loop(1, 8, send, 0)
        keep(number).start()

    az1.leave()
    az2.step(0)
    by.step(0)
    az1.step(1)
    az2.step(1)
    by.step(1)
    az1.step(2)
    az2.step(2)
    az1.step(3)
    az2.step(3)
    by.arrive()
    bz1.step(0)
    az1.arrive()
    ay1.step(0)
    bz2.step(0)
    az2.arrive()
    ay1.step(1)
    ay2.step(0)
    bz1.step(1)
    bz2.step(1)
    ay1.arrive()
    deliver(8, 0, ay1)
    ay2.step(1)
    bz1.step(2)
    bz2.step(2)
    ay2.arrive()
    deliver(8, 1, ay2)
    bz1.step(3)
    bz2.step(3)
    bz1.arrive()
    deliver(9, 2, bz1)
    bz2.arrive()
    deliver(9, 3, bz2)
    for number in range(4):

        def settle(k, carry):
            spread(number, k).wait_recv()
            return carry

        lax.fori_loop(1, 8, settle, 0)
        pltpu.make_async_remote_copy(
            src_ref=packs.at[number, pl.ds(0, 21)],
            dst_ref=packs.at[number, pl.ds(0, 21)],
            send_sem=mp_send.at[number],
            recv_sem=mp_recv.at[number, 1],
            device_id=(dp, (mp + 1) % 8),
            device_id_type=MESH,
        ).wait_send()
        keep(number).wait()
    for lanes in (by, az1, az2, ay1, ay2, bz1, bz2):
        lanes.close()


def exchange(number, table, grads):
    steps_z, steps_y = BUILDS[number]
    held, rows, columns = grads.shape

    def buffers(steps, parts):
        return [pltpu.VMEM((4 * steps, rows, columns // parts), jnp.bfloat16)] * 2

    def sems(*steps):
        return [pltpu.SemaphoreType.DMA((size,)) for count in steps for size in (1, 2 * count)]

    return pl.pallas_call(
        functools.partial(exchange_kernel, steps_z, steps_y),
        out_shape=jax.ShapeDtypeStruct((3, columns, columns), jnp.bfloat16),
        in_specs=[pl.BlockSpec(memory_space=pltpu.SMEM), pl.BlockSpec(memory_space=pl.ANY)],
        out_specs=pl.BlockSpec(memory_space=pl.ANY),
        scratch_shapes=[pltpu.VMEM(grads.shape, jnp.bfloat16)]
        + buffers(steps_y, 2)
        + buffers(steps_z, 4) * 2
        + buffers(steps_y, 4) * 2
        + buffers(steps_z, 4) * 2
        + [pltpu.VMEM((4, held, rows, columns // 4), jnp.bfloat16)]
        + sems(steps_y, steps_z, steps_z, steps_y, steps_y, steps_z, steps_z)
        + [pltpu.SemaphoreType.DMA((4,)), pltpu.SemaphoreType.DMA((4, 8)), pltpu.SemaphoreType.DMA((5,))],
        compiler_params=pltpu.CompilerParams(
            collective_id=1 + number, has_side_effects=True, vmem_limit_bytes=56 << 20
        ),
        name=f"exchange_{steps_z}_{steps_y}",
    )(table, grads)


def newton_root(matrix):
    size = matrix.shape[0]
    identity = (
        lax.broadcasted_iota(jnp.int32, (size, size), 0) == lax.broadcasted_iota(jnp.int32, (size, size), 1)
    ).astype(jnp.float32)
    wide = matrix.astype(jnp.float32)
    scaling = 2.5 / jnp.sqrt(jnp.sum(wide * wide) + 1e-06)
    scaled = scaling * wide
    squared = (scaling * scaling) * multiply(matrix, matrix)
    shift = (squared - 10.0 * scaled) * 0.0625
    half_shift = shift.astype(jnp.bfloat16)
    quartic = 3.125 * shift + multiply(half_shift, half_shift)
    through = (5.0 * scaled - squared) * 0.25
    fifth = 2.44140625 * through + multiply(quartic.astype(jnp.bfloat16), through.astype(jnp.bfloat16))
    offset = -0.3125 * scaled - 0.25 * fifth
    half_offset = offset.astype(jnp.bfloat16)
    doubled = 3.125 * offset + multiply(half_offset, half_offset)
    half_doubled = doubled.astype(jnp.bfloat16)
    fourth = 4.8828125 * doubled + multiply(half_doubled, half_doubled)
    carried = 1.5625 * scaled + scaling * multiply(half_offset, matrix)
    last = 5.9604644775390625 * carried + multiply(fourth.astype(jnp.bfloat16), carried.astype(jnp.bfloat16))
    root = 1.953125 * identity + 1.25 * offset - 0.25 * last
    return (jnp.sqrt(jnp.sqrt(scaling)) * root).astype(jnp.bfloat16)


def update_kernel(flag_ref, grad_ref, left_ref, right_ref, left_root_ref, right_root_ref, left_out, right_out, dir_out, use_left, use_right):
    slot = pl.program_id(0)
    block = grad_ref[0]
    gram_left = lax.dot_general(block, block, (((1,), (1,)), ((), ())), preferred_element_type=jnp.float32)
    left_out[0] = (decay_rate * left_ref[0].astype(jnp.float32) + (1.0 - decay_rate) * gram_left).astype(jnp.bfloat16)
    gram_right = lax.dot_general(block, block, (((0,), (0,)), ((), ())), preferred_element_type=jnp.float32)
    right_out[0] = (decay_rate * right_ref[0].astype(jnp.float32) + (1.0 - decay_rate) * gram_right).astype(jnp.bfloat16)

    @pl.when(flag_ref[slot] > 0)
    def _():
        use_left[...] = newton_root(left_out[0])
        use_right[...] = newton_root(right_out[0])

    @pl.when(flag_ref[slot] <= 0)
    def _():
        use_left[...] = left_root_ref[0]
        use_right[...] = right_root_ref[0]

    half_way = multiply(use_left[...], block).astype(jnp.bfloat16)
    preconditioned = multiply(half_way, use_right[...])
    wide = block.astype(jnp.float32)
    grad_norm = jnp.sum(wide * wide)
    dir_norm = jnp.sum(preconditioned * preconditioned)
    dir_out[0] = (preconditioned * jnp.sqrt(grad_norm / (dir_norm + 1e-06))).astype(jnp.bfloat16)


def update(refresh_flag, blocks, left_stats, right_stats, left_root, right_root):
    slots, size = blocks.shape[0], blocks.shape[1]
    spec = pl.BlockSpec((1, size, size), lambda k: (k, 0, 0))
    return pl.pallas_call(
        update_kernel,
        grid=(slots,),
        in_specs=[pl.BlockSpec(memory_space=pltpu.SMEM)] + [spec] * 5,
        out_specs=[spec] * 3,
        out_shape=[jax.ShapeDtypeStruct(blocks.shape, jnp.bfloat16)] * 3,
        scratch_shapes=[pltpu.VMEM((size, size), jnp.bfloat16)] * 2,
        compiler_params=pltpu.CompilerParams(vmem_limit_bytes=56 << 20),
        name="update",
    )(refresh_flag, blocks, left_stats, right_stats, left_root, right_root)


def local(grads, owner_slot, refresh_flag, left_stats, right_stats, left_root, right_root):
    table, build = make_plan(owner_slot)
    builds = [functools.partial(exchange, number) for number in range(len(BUILDS))]
    blocks = lax.switch(build[0, 0], builds, table, grads)
    return tuple(update(refresh_flag, blocks, left_stats, right_stats, left_root, right_root))


def solution(mesh):
    placed = (
        P("dp", "mp", None),
        P("dp"),
        P(("dp", "mp")),
        P(("dp", "mp"), None, None),
        P(("dp", "mp"), None, None),
        P(("dp", "mp"), None, None),
        P(("dp", "mp"), None, None),
    )
    return jax.shard_map(
        local,
        mesh=mesh,
        in_specs=placed,
        out_specs=(
            P(("dp", "mp"), None, None),
            P(("dp", "mp"), None, None),
            P(("dp", "mp"), None, None),
        ),
        check_vma=False,
    )
```

```python
import functools

import jax
import jax.numpy as jnp
from jax import lax
from jax.experimental import pallas as pl
from jax.experimental.pallas import tpu as pltpu
from jax.sharding import PartitionSpec as P

decay_rate = 0.9


def multiply(first_op, second_op):
    return jnp.dot(first_op, second_op, preferred_element_type=jnp.float32)


def iota2(shape, axis):
    return lax.broadcasted_iota(jnp.int32, shape, axis)


def total_of(mask, values):
    return jnp.max(jnp.where(mask, values, 0), keepdims=True)


def long_need(ones, twos, threes, fours):
    odd = twos & 1
    rest = jnp.maximum(ones - threes - 2 * odd, 0)
    lanes = fours + threes + ((twos + 1) >> 1) + ((rest + 3) >> 2)
    spare = ones - threes
    used = jnp.where(
        rest > 0,
        jnp.where((rest & 3) == 0, 4, rest & 3),
        jnp.where(
            twos > 0,
            jnp.where(odd == 1, 2 + jnp.clip(spare, 0, 2), 4),
            jnp.where(threes > 0, jnp.where(spare >= 0, 4, 3), 4),
        ),
    )
    return jnp.where(lanes > 0, 4 * (lanes - 1) + used, 0)


def long_share(counts):
    n1, n2, n3, n4, n5, n6, n7 = counts
    best, split = jnp.maximum(long_need(n1, n2, n3, 0 * n4), long_need(n7, n6, n5, n4)), 0 * n4
    for c in range(1, 5):
        other = jnp.maximum(long_need(n1, n2, n3, 0 * n4 + c), long_need(n7, n6, n5, jnp.maximum(n4 - c, 0)))
        better = (n4 >= c) & (other < best)
        best, split = jnp.where(better, other, best), jnp.where(better, c, split)
    return split, best


def long_plan(counts, split, hop, rank):
    n1, n2, n3, n4, n5, n6, n7 = counts
    plus = (hop < 4) | ((hop == 4) & (rank < split))
    length = jnp.where(plus, hop, 8 - hop)
    index = jnp.where((hop == 4) & (rank >= split), rank - split, rank)
    twos, threes = jnp.where(plus, n2, n6), jnp.where(plus, n3, n5)
    fours = jnp.where(plus, split, n4 - split)
    odd = twos & 1
    spare = index - threes
    rest = spare - 2 * odd
    lane1 = jnp.where(
        spare < 0,
        fours + index,
        jnp.where(rest < 0, fours + threes + (twos >> 1), fours + threes + ((twos + 1) >> 1) + (rest >> 2)),
    )
    start1 = jnp.where(spare < 0, 3, jnp.where(rest < 0, 2 + spare, rest & 3))
    lane = jnp.where(
        length == 4,
        index,
        jnp.where(length == 3, fours + index, jnp.where(length == 2, fours + threes + (index >> 1), lane1)),
    )
    start = jnp.where(length >= 3, 0, jnp.where(length == 2, 2 * (index & 1), start1))
    first = jnp.where(plus, 0, 32) + 4 * lane + start
    return first, first + length - 1


def short_share(counts):
    m1, m2, m3 = counts
    best, split = jnp.maximum(m1, 2 * m2 + m3), 0 * m2
    for c in range(1, 9):
        other = jnp.maximum(2 * c + m1, 2 * (m2 - c) + m3)
        better = (m2 >= c) & (other < best)
        best, split = jnp.where(better, other, best), jnp.where(better, c, split)
    return split, best


def short_plan(counts, split, hop, rank):
    m1, m2, m3 = counts
    plus = (hop == 1) | ((hop == 2) & (rank < split))
    index = jnp.where((hop == 2) & (rank >= split), rank - split, rank)
    twos = jnp.where(plus, split, m2 - split)
    lane = jnp.where(hop == 2, index, twos + (index >> 1))
    start = jnp.where(hop == 2, 0, index & 1)
    first = jnp.where(plus, 0, 16) + 2 * lane + start
    return first, first + jnp.where(hop == 2, 1, 0)


def plan(owner, me):
    square = (32, 32)
    source, target = iota2(square, 0), iota2(square, 1)
    ys, zs, yt, zt = source >> 3, source & 7, target >> 3, target & 7
    along_y, along_z = (yt - ys) & 3, (zt - zs) & 7
    both, later = jnp.zeros(square, jnp.int32), jnp.full(square, -1, jnp.int32)
    for b in range(24):
        inside = owner[:, b : b + 1] - 24 * target
        match = (inside >= 0) & (inside < 24)
        entry = inside + 32 * b
        both = both + jnp.where(match, entry, 0)
        later = jnp.where(match, entry, later)
    present = later >= 0
    entries = [both - later, later]
    held, label = [entry >> 5 for entry in entries], [entry & 31 for entry in entries]
    flags = jnp.where(present, 1.0, 0.0).astype(jnp.bfloat16)

    def count(first_op, second_op):
        return jnp.dot(first_op, second_op, preferred_element_type=jnp.float32).astype(jnp.int32)

    def mask(condition):
        return jnp.where(condition, 1.0, 0.0).astype(jnp.bfloat16)

    same_z, same_y = zs == zt, ys == yt
    rank_az, many_az = count(flags, mask(same_z & (ys < yt))), count(flags, mask(same_z))
    rank_by, many_by = count(flags, mask(same_y & (zs < zt))), count(flags, mask(same_y))
    rank_ay, many_ay = count(mask(same_y & (zt < zs)), flags), count(mask(same_y), flags)
    rank_bz, many_bz = count(mask(same_z & (yt < ys)), flags), count(mask(same_z), flags)
    many_z, many_y = jnp.maximum(many_az, many_bz), jnp.maximum(many_ay, many_by)
    counts_z = [total_of(along_z == k, many_z) for k in range(1, 8)]
    counts_y = [total_of(along_y == k, many_y) for k in range(1, 4)]
    split_z, need_z = long_share(counts_z)
    split_y, need_y = short_share(counts_y)
    first_az, last_az = long_plan(counts_z, split_z, along_z, rank_az)
    first_bz, last_bz = long_plan(counts_z, split_z, along_z, rank_bz)
    first_ay, last_ay = short_plan(counts_y, split_y, along_y, rank_ay)
    first_by, last_by = short_plan(counts_y, split_y, along_y, rank_by)

    lanes = iota2((1, 64), 1)
    diagonal = source == target

    def standing(row):
        return jnp.sum(jnp.where(diagonal, row, 0), axis=1, keepdims=True)

    def table(place, values):
        at, value = standing(place), standing(values)
        return jnp.sum(jnp.where(at == lanes, value + 1, 0), axis=0, keepdims=True) - 1

    def own_row(values):
        return jnp.sum(jnp.where(source == me, values, 0), axis=0, keepdims=True)

    my_y, my_z = me >> 3, me & 7
    rows = []
    place = own_row(jnp.where(present & (along_z > 0), first_az, -1))
    rows += [table(place, own_row(held[p])) for p in range(2)]
    place = own_row(jnp.where(present & (along_y > 0), first_by, -1))
    rows += [table(place, own_row(held[p])) for p in range(2)]

    spread_y, spread_z = mask(ys == yt), mask(zs == zt)

    def condense(keep, values, spread, pick):
        moved = count(jnp.where(keep, values, 0).astype(jnp.float32).astype(jnp.bfloat16), spread)
        return jnp.sum(jnp.where(pick, moved, 0), axis=0, keepdims=True)

    keep = present & (along_y > 0) & (ys == my_y) & (zt == my_z)
    pick = (ys == my_y) & (zs == zt)
    place = condense(keep, first_ay + 1, spread_y, pick) - 1
    for p in range(2):
        code = jnp.where(along_z == 0, held[p], 32 + last_az)
        rows.append(table(place, condense(keep, code, spread_y, pick)))
    keep = present & (along_z > 0) & (zs == my_z) & (yt == my_y)
    pick = (zs == my_z) & (ys == yt)
    place = condense(keep, first_bz + 1, spread_z, pick) - 1
    for p in range(2):
        code = jnp.where(along_y == 0, held[p], 32 + last_by)
        rows.append(table(place, condense(keep, code, spread_z, pick)))

    def column(values):
        return jnp.sum(jnp.where(target == me, values, 0), axis=1, keepdims=True)

    for first_axis, second_axis, last_one, last_two in ((along_z, along_y, last_az, last_ay), (along_y, along_z, last_by, last_bz)):
        row = jnp.zeros((1, 64), jnp.int32)
        for p in range(2):
            code = jnp.where(
                second_axis > 0,
                160 + 2 * last_two + p,
                jnp.where(first_axis > 0, 32 + 2 * last_one + p, held[p]),
            )
            at, value = column(jnp.where(present, label[p] + 1, 0)) - 1, column(code)
            row = row + jnp.sum(jnp.where(at == lanes, value, 0), axis=0, keepdims=True)
        rows.append(row)
    return rows, need_z, need_y


MESH = pl.DeviceIdType.MESH
BUILDS = ((10, 9), (12, 9), (14, 9), (14, 11), (16, 11), (32, 16))


def along(axis, distance):
    dp = lax.axis_index("dp")
    if axis == "z":
        return ((dp // 8) * 8 + (dp + distance) % 8, lax.axis_index("mp"))
    return ((dp + 8 * distance) % 32, lax.axis_index("mp"))


def meet(devices):
    barrier = pltpu.get_barrier_semaphore()
    for device in devices:
        pl.semaphore_signal(barrier, inc=1, device_id=device, device_id_type=MESH)
    pl.semaphore_wait(barrier, len(devices))


def plan_kernel(slots_ref, table_ref, build_ref, owner, send_sem, recv_sem):
    dp = lax.axis_index("dp")
    row = dp // 8
    ring_z = [along("z", k) for k in range(1, 8)]
    ring_y = [along("y", k) for k in range(1, 4)]
    owner[pl.ds(dp, 1), :, 0 : slots_ref.shape[2]] = slots_ref[...]
    meet(ring_z + ring_y)
    copies = []
    for k, device in enumerate(ring_z):
        copies.append(
            pltpu.make_async_remote_copy(
                src_ref=owner.at[pl.ds(dp, 1)],
                dst_ref=owner.at[pl.ds(dp, 1)],
                send_sem=send_sem.at[k],
                recv_sem=recv_sem.at[k],
                device_id=device,
                device_id_type=MESH,
            )
        )
        copies[-1].start()
    for copy in copies:
        copy.wait_recv()
    for k, device in enumerate(ring_y):
        copies.append(
            pltpu.make_async_remote_copy(
                src_ref=owner.at[pl.ds(8 * row, 8)],
                dst_ref=owner.at[pl.ds(8 * row, 8)],
                send_sem=send_sem.at[7 + k],
                recv_sem=recv_sem.at[7 + k],
                device_id=device,
                device_id_type=MESH,
            )
        )
        copies[-1].start()
    for copy in copies[7:]:
        copy.wait_recv()
    for copy in copies:
        copy.wait_send()
    rows, need_z, need_y = plan(owner[...].reshape(32, 128), dp)
    for k, entries in enumerate(rows):
        table_ref[k : k + 1, 0:64] = entries
    build = jnp.full((1, 1), len(BUILDS) - 1, jnp.int32)
    for number in range(len(BUILDS) - 2, -1, -1):
        steps_z, steps_y = BUILDS[number]
        build = jnp.where((need_z <= steps_z) & (need_y <= steps_y), number, build)
    build_ref[...] = build


def make_plan(owner_slot):
    slots = owner_slot.reshape(1, 1, owner_slot.shape[0])
    vmem = pl.BlockSpec(memory_space=pltpu.VMEM)
    return pl.pallas_call(
        plan_kernel,
        out_shape=[jax.ShapeDtypeStruct((16, 128), jnp.int32), jax.ShapeDtypeStruct((1, 1), jnp.int32)],
        in_specs=[vmem],
        out_specs=[vmem, vmem],
        scratch_shapes=[
            pltpu.VMEM((32, 1, 128), jnp.int32),
            pltpu.SemaphoreType.DMA((10,)),
            pltpu.SemaphoreType.DMA((10,)),
        ],
        compiler_params=pltpu.CompilerParams(collective_id=0, has_side_effects=True),
        name="plan",
    )(slots)


class Lanes:
    def __init__(self, near, steps, rows, columns, table, own, before, buffers, sems):
        self.near, self.length, self.half = near
        self.steps, self.rows, self.columns = steps, rows, columns
        self.table, self.own, self.before = table, own, before
        self.sent, self.got = buffers
        self.send_sem, self.recv_sem = sems

    def received(self, entry, columns):
        unused = jnp.where(entry >= 2 * self.half, 2 * (self.half - self.steps), 0)
        return self.got[jnp.clip(entry - unused, 0, 4 * self.steps - 1), :, columns]

    def value(self, way, at, p, step):
        code = self.table[self.rows + p, way * self.half + at]
        fresh = self.own[jnp.clip(code, 0, 23), :, self.columns]
        if self.before is not None:
            lanes, columns = self.before
            fresh = jnp.where(code < 32, fresh, lanes.received(2 * (code - 32) + p, columns))
        if step == 0:
            return fresh
        return jnp.where(code >= 0, fresh, self.got[2 * (way * self.steps + at - 1) + p])

    def copy(self, way, at):
        plus, minus = self.near
        place = way * self.steps + at
        return pltpu.make_async_remote_copy(
            src_ref=self.sent.at[pl.ds(2 * place, 2)],
            dst_ref=self.got.at[pl.ds(2 * place, 2)],
            send_sem=self.send_sem.at[0],
            recv_sem=self.recv_sem.at[place],
            device_id=(plus + way * (minus - plus), lax.axis_index("mp")),
            device_id_type=MESH,
        )

    def each(self, step, action):
        lanes = (self.steps - step + self.length - 1) // self.length

        def body(number, carry):
            action(number % 2, number // 2 * self.length + step)
            return carry

        lax.fori_loop(0, 2 * lanes, body, 0)

    def fill(self, way, at, step):
        for p in range(2):
            self.sent[2 * (way * self.steps + at) + p] = self.value(way, at, p, step)

    def ready(self):
        self.each(0, lambda way, at: self.fill(way, at, 0))

    def leave(self):
        self.each(0, lambda way, at: self.copy(way, at).start())

    def step(self, step):
        def action(way, at):
            if step > 0:
                self.copy(way, at - 1).wait_recv()
            self.fill(way, at, step)
            self.copy(way, at).start()

        self.each(step, action)

    def arrive(self):
        whole, part = self.steps // self.length, self.steps % self.length

        def body(number, carry):
            lane = number // 2
            last = jnp.where(lane < whole, self.length, part) - 1
            self.copy(number % 2, lane * self.length + last).wait_recv()
            return carry

        lax.fori_loop(0, 2 * (whole + (part > 0)), body, 0)

    def close(self):
        pltpu.make_async_remote_copy(
            src_ref=self.sent,
            dst_ref=self.got,
            send_sem=self.send_sem.at[0],
            recv_sem=self.recv_sem.at[0],
            device_id=(self.near[0], lax.axis_index("mp")),
            device_id_type=MESH,
        ).wait_send()


def exchange_kernel(steps_z, steps_y, table, grads, blocks, own, *scratch):
    buffers_by = scratch[0:2]
    buffers_az, buffers_ay, buffers_bz = ((scratch[k : k + 2], scratch[k + 2 : k + 4]) for k in (2, 6, 10))
    packs = scratch[14]
    sems = [(scratch[15 + 2 * k], scratch[16 + 2 * k]) for k in range(7)]
    mp_send, mp_recv, local_sem = scratch[29:]
    mp = lax.axis_index("mp")
    dp = lax.axis_index("dp")
    load = pltpu.make_async_copy(grads, own, local_sem.at[4])
    load.start()
    barrier = pltpu.get_barrier_semaphore()
    row = (dp // 8) * 8
    near_z = (row + (dp + 1) % 8, row + (dp + 7) % 8)
    near_y = ((dp + 8) % 32, (dp + 24) % 32)
    for device in near_z + near_y:
        pl.semaphore_signal(barrier, inc=1, device_id=(device, mp), device_id_type=MESH)

    def greet(k, carry):
        pl.semaphore_signal(barrier, inc=1, device_id=(dp, (mp + k) % 8), device_id_type=MESH)
        return carry

    lax.fori_loop(1, 8, greet, 0)
    half = own.shape[2] // 2
    quarter = half // 2
    quarters = [pl.ds(k * quarter, quarter) for k in range(4)]
    by = Lanes((near_y, 2, 16), steps_y, 2, pl.ds(half, half), table, own, None, buffers_by, sems[0])
    az1, az2 = (
        Lanes((near_z, 4, 32), steps_z, 0, quarters[k], table, own, None, buffers_az[k], sems[1 + k])
        for k in range(2)
    )
    ay1, ay2 = (
        Lanes((near_y, 2, 16), steps_y, 4, quarters[k], table, own, ((az1, az2)[k], quarters[0]), buffers_ay[k], sems[3 + k])
        for k in range(2)
    )
    bz1, bz2 = (
        Lanes((near_z, 4, 32), steps_z, 6, quarters[2 + k], table, own, (by, quarters[k]), buffers_bz[k], sems[5 + k])
        for k in range(2)
    )
    load.wait()
    az1.ready()
    pl.semaphore_wait(barrier, 11)

    def place(number):
        return blocks.at[:, pl.ds(pl.multiple_of(64 * mp, 64), 64), quarters[number]]

    def spread(number, k):
        peer = (mp + k) % 8
        return pltpu.make_async_remote_copy(
            src_ref=packs.at[number, pl.ds(3 * peer, 3)],
            dst_ref=place(number),
            send_sem=mp_send.at[number],
            recv_sem=mp_recv.at[number, k],
            device_id=(dp, peer),
            device_id_type=MESH,
        )

    def keep(number):
        return pltpu.make_async_copy(packs.at[number, pl.ds(3 * mp, 3)], place(number), local_sem.at[number])

    def deliver(row, number, lanes):
        columns = quarters[number]
        first, first_columns = lanes.before

        def sort(peer):
            for k in range(3):
                slot = 3 * peer + k
                code = table[row, slot]
                packs[number, slot] = jnp.where(
                    code < 32,
                    own[jnp.clip(code, 0, 23), :, columns],
                    jnp.where(
                        code < 160,
                        first.received(code - 32, first_columns),
                        lanes.received(code - 160, quarters[0]),
                    ),
                )

        def send(k, carry):
            sort((mp + k) % 8)
            spread(number, k).start()
            return carry

        lax.fori_loop(1, 8, send, 0)
        sort(mp)
        keep(number).start()

    az1.leave()
    az2.step(0)
    by.step(0)
    az1.step(1)
    az2.step(1)
    by.step(1)
    az1.step(2)
    az2.step(2)
    az1.step(3)
    az2.step(3)
    by.arrive()
    bz1.step(0)
    az1.arrive()
    ay1.step(0)
    bz2.step(0)
    az2.arrive()
    ay1.step(1)
    ay2.step(0)
    bz1.step(1)
    bz2.step(1)
    ay1.arrive()
    deliver(8, 0, ay1)
    ay2.step(1)
    bz1.step(2)
    bz2.step(2)
    ay2.arrive()
    deliver(8, 1, ay2)
    bz1.step(3)
    bz2.step(3)
    bz1.arrive()
    deliver(9, 2, bz1)
    bz2.arrive()
    deliver(9, 3, bz2)
    for number in range(4):

        def settle(k, carry):
            spread(number, k).wait_recv()
            return carry

        lax.fori_loop(1, 8, settle, 0)
        pltpu.make_async_remote_copy(
            src_ref=packs.at[number, pl.ds(0, 21)],
            dst_ref=packs.at[number, pl.ds(0, 21)],
            send_sem=mp_send.at[number],
            recv_sem=mp_recv.at[number, 1],
            device_id=(dp, (mp + 1) % 8),
            device_id_type=MESH,
        ).wait_send()
        keep(number).wait()
    for lanes in (by, az1, az2, ay1, ay2, bz1, bz2):
        lanes.close()


def exchange(number, table, grads):
    steps_z, steps_y = BUILDS[number]
    held, rows, columns = grads.shape

    def buffers(steps, parts):
        return [pltpu.VMEM((4 * steps, rows, columns // parts), jnp.bfloat16)] * 2

    def sems(*steps):
        return [pltpu.SemaphoreType.DMA((size,)) for count in steps for size in (1, 2 * count)]

    return pl.pallas_call(
        functools.partial(exchange_kernel, steps_z, steps_y),
        out_shape=jax.ShapeDtypeStruct((3, columns, columns), jnp.bfloat16),
        in_specs=[pl.BlockSpec(memory_space=pltpu.SMEM), pl.BlockSpec(memory_space=pl.ANY)],
        out_specs=pl.BlockSpec(memory_space=pl.ANY),
        scratch_shapes=[pltpu.VMEM(grads.shape, jnp.bfloat16)]
        + buffers(steps_y, 2)
        + buffers(steps_z, 4) * 2
        + buffers(steps_y, 4) * 2
        + buffers(steps_z, 4) * 2
        + [pltpu.VMEM((4, held, rows, columns // 4), jnp.bfloat16)]
        + sems(steps_y, steps_z, steps_z, steps_y, steps_y, steps_z, steps_z)
        + [pltpu.SemaphoreType.DMA((4,)), pltpu.SemaphoreType.DMA((4, 8)), pltpu.SemaphoreType.DMA((5,))],
        compiler_params=pltpu.CompilerParams(
            collective_id=1 + number, has_side_effects=True, vmem_limit_bytes=56 << 20
        ),
        name=f"exchange_{steps_z}_{steps_y}",
    )(table, grads)


def newton_roots(*matrices):
    size = matrices[0].shape[0]
    diagonal = lax.broadcasted_iota(jnp.int32, (size, size), 0) == lax.broadcasted_iota(jnp.int32, (size, size), 1)

    def narrow(values):
        return [value.astype(jnp.bfloat16) for value in values]

    def products(first_ops, second_ops):
        return [multiply(one, two) for one, two in zip(first_ops, second_ops)]

    wide = [matrix.astype(jnp.float32) for matrix in matrices]
    scalings = [2.5 / jnp.sqrt(jnp.sum(value * value) + 1e-06) for value in wide]
    scaled = [scaling * value for scaling, value in zip(scalings, wide)]
    squared = [(scaling * scaling) * value for scaling, value in zip(scalings, products(matrices, matrices))]
    shift = [(two - 10.0 * one) * 0.0625 for one, two in zip(scaled, squared)]
    through = [(5.0 * one - two) * 0.25 for one, two in zip(scaled, squared)]
    half_shift = narrow(shift)
    quartic = [3.125 * one + two for one, two in zip(shift, products(half_shift, half_shift))]
    fifth = [2.44140625 * one + two for one, two in zip(through, products(narrow(quartic), narrow(through)))]
    offset = [-0.3125 * one - 0.25 * two for one, two in zip(scaled, fifth)]
    half_offset = narrow(offset)
    doubled = [3.125 * one + two for one, two in zip(offset, products(half_offset, half_offset))]
    half_doubled = narrow(doubled)
    carried = [
        1.5625 * one + scaling * two for scaling, one, two in zip(scalings, scaled, products(half_offset, matrices))
    ]
    fourth = [4.8828125 * one + two for one, two in zip(doubled, products(half_doubled, half_doubled))]
    last = [5.9604644775390625 * one + two for one, two in zip(carried, products(narrow(fourth), narrow(carried)))]
    return [
        (jnp.sqrt(jnp.sqrt(scaling)) * (jnp.where(diagonal, 1.953125, 0.0) + 1.25 * one - 0.25 * two)).astype(jnp.bfloat16)
        for scaling, one, two in zip(scalings, offset, last)
    ]


def update_kernel(flag_ref, grad_ref, left_ref, right_ref, left_root_ref, right_root_ref, left_out, right_out, dir_out, use_left, use_right):
    slot = pl.program_id(0)
    block = grad_ref[0]
    gram_left = lax.dot_general(block, block, (((1,), (1,)), ((), ())), preferred_element_type=jnp.float32)
    left_out[0] = (decay_rate * left_ref[0].astype(jnp.float32) + (1.0 - decay_rate) * gram_left).astype(jnp.bfloat16)
    gram_right = lax.dot_general(block, block, (((0,), (0,)), ((), ())), preferred_element_type=jnp.float32)
    right_out[0] = (decay_rate * right_ref[0].astype(jnp.float32) + (1.0 - decay_rate) * gram_right).astype(jnp.bfloat16)

    @pl.when(flag_ref[slot] > 0)
    def _():
        use_left[...], use_right[...] = newton_roots(left_out[0], right_out[0])

    @pl.when(flag_ref[slot] <= 0)
    def _():
        use_left[...] = left_root_ref[0]
        use_right[...] = right_root_ref[0]

    half_way = multiply(use_left[...], block).astype(jnp.bfloat16)
    preconditioned = multiply(half_way, use_right[...])
    wide = block.astype(jnp.float32)
    grad_norm = jnp.sum(wide * wide)
    dir_norm = jnp.sum(preconditioned * preconditioned)
    dir_out[0] = (preconditioned * jnp.sqrt(grad_norm / (dir_norm + 1e-06))).astype(jnp.bfloat16)


def update(refresh_flag, blocks, left_stats, right_stats, left_root, right_root):
    slots, size = blocks.shape[0], blocks.shape[1]
    spec = pl.BlockSpec((1, size, size), lambda k: (k, 0, 0))
    return pl.pallas_call(
        update_kernel,
        grid=(slots,),
        in_specs=[pl.BlockSpec(memory_space=pltpu.SMEM)] + [spec] * 5,
        out_specs=[spec] * 3,
        out_shape=[jax.ShapeDtypeStruct(blocks.shape, jnp.bfloat16)] * 3,
        scratch_shapes=[pltpu.VMEM((size, size), jnp.bfloat16)] * 2,
        compiler_params=pltpu.CompilerParams(vmem_limit_bytes=56 << 20),
        name="update",
    )(refresh_flag, blocks, left_stats, right_stats, left_root, right_root)


def local(grads, owner_slot, refresh_flag, left_stats, right_stats, left_root, right_root):
    table, build = make_plan(owner_slot)
    builds = [functools.partial(exchange, number) for number in range(len(BUILDS))]
    blocks = lax.switch(build[0, 0], builds, table, grads)
    return tuple(update(refresh_flag, blocks, left_stats, right_stats, left_root, right_root))


def solution(mesh):
    placed = (
        P("dp", "mp", None),
        P("dp"),
        P(("dp", "mp")),
        P(("dp", "mp"), None, None),
        P(("dp", "mp"), None, None),
        P(("dp", "mp"), None, None),
        P(("dp", "mp"), None, None),
    )
    return jax.shard_map(
        local,
        mesh=mesh,
        in_specs=placed,
        out_specs=(
            P(("dp", "mp"), None, None),
            P(("dp", "mp"), None, None),
            P(("dp", "mp"), None, None),
        ),
        check_vma=False,
    )
```

```python
import functools

import jax
import jax.numpy as jnp
from jax import lax
from jax.experimental import pallas as pl
from jax.experimental.pallas import tpu as pltpu
from jax.sharding import PartitionSpec as P

decay_rate = 0.9


def multiply(first_op, second_op):
    return jnp.dot(first_op, second_op, preferred_element_type=jnp.float32)


def iota2(shape, axis):
    return lax.broadcasted_iota(jnp.int32, shape, axis)


def total_of(mask, values):
    return jnp.max(jnp.where(mask, values, 0), keepdims=True)


def long_need(ones, twos, threes, fours):
    odd = twos & 1
    rest = jnp.maximum(ones - threes - 2 * odd, 0)
    lanes = fours + threes + ((twos + 1) >> 1) + ((rest + 3) >> 2)
    spare = ones - threes
    used = jnp.where(
        rest > 0,
        jnp.where((rest & 3) == 0, 4, rest & 3),
        jnp.where(
            twos > 0,
            jnp.where(odd == 1, 2 + jnp.clip(spare, 0, 2), 4),
            jnp.where(threes > 0, jnp.where(spare >= 0, 4, 3), 4),
        ),
    )
    return jnp.where(lanes > 0, 4 * (lanes - 1) + used, 0)


def long_share(counts):
    n1, n2, n3, n4, n5, n6, n7 = counts
    best, split = jnp.maximum(long_need(n1, n2, n3, 0 * n4), long_need(n7, n6, n5, n4)), 0 * n4
    for c in range(1, 5):
        other = jnp.maximum(long_need(n1, n2, n3, 0 * n4 + c), long_need(n7, n6, n5, jnp.maximum(n4 - c, 0)))
        better = (n4 >= c) & (other < best)
        best, split = jnp.where(better, other, best), jnp.where(better, c, split)
    return split, best


def long_plan(counts, split, hop, rank):
    n1, n2, n3, n4, n5, n6, n7 = counts
    plus = (hop < 4) | ((hop == 4) & (rank < split))
    length = jnp.where(plus, hop, 8 - hop)
    index = jnp.where((hop == 4) & (rank >= split), rank - split, rank)
    twos, threes = jnp.where(plus, n2, n6), jnp.where(plus, n3, n5)
    fours = jnp.where(plus, split, n4 - split)
    odd = twos & 1
    spare = index - threes
    rest = spare - 2 * odd
    lane1 = jnp.where(
        spare < 0,
        fours + index,
        jnp.where(rest < 0, fours + threes + (twos >> 1), fours + threes + ((twos + 1) >> 1) + (rest >> 2)),
    )
    start1 = jnp.where(spare < 0, 3, jnp.where(rest < 0, 2 + spare, rest & 3))
    lane = jnp.where(
        length == 4,
        index,
        jnp.where(length == 3, fours + index, jnp.where(length == 2, fours + threes + (index >> 1), lane1)),
    )
    start = jnp.where(length >= 3, 0, jnp.where(length == 2, 2 * (index & 1), start1))
    first = jnp.where(plus, 0, 32) + 4 * lane + start
    return first, first + length - 1


def short_share(counts):
    m1, m2, m3 = counts
    best, split = jnp.maximum(m1, 2 * m2 + m3), 0 * m2
    for c in range(1, 9):
        other = jnp.maximum(2 * c + m1, 2 * (m2 - c) + m3)
        better = (m2 >= c) & (other < best)
        best, split = jnp.where(better, other, best), jnp.where(better, c, split)
    return split, best


def short_plan(counts, split, hop, rank):
    m1, m2, m3 = counts
    plus = (hop == 1) | ((hop == 2) & (rank < split))
    index = jnp.where((hop == 2) & (rank >= split), rank - split, rank)
    twos = jnp.where(plus, split, m2 - split)
    lane = jnp.where(hop == 2, index, twos + (index >> 1))
    start = jnp.where(hop == 2, 0, index & 1)
    first = jnp.where(plus, 0, 16) + 2 * lane + start
    return first, first + jnp.where(hop == 2, 1, 0)


def plan(owner, me):
    square = (32, 32)
    source, target = iota2(square, 0), iota2(square, 1)
    ys, zs, yt, zt = source >> 3, source & 7, target >> 3, target & 7
    along_y, along_z = (yt - ys) & 3, (zt - zs) & 7
    both, later = jnp.zeros(square, jnp.int32), jnp.full(square, -1, jnp.int32)
    for b in range(24):
        inside = owner[:, b : b + 1] - 24 * target
        match = (inside >= 0) & (inside < 24)
        entry = inside + 32 * b
        both = both + jnp.where(match, entry, 0)
        later = jnp.where(match, entry, later)
    present = later >= 0
    entries = [both - later, later]
    held, label = [entry >> 5 for entry in entries], [entry & 31 for entry in entries]
    flags = jnp.where(present, 1.0, 0.0).astype(jnp.bfloat16)

    def count(first_op, second_op):
        return jnp.dot(first_op, second_op, preferred_element_type=jnp.float32).astype(jnp.int32)

    def mask(condition):
        return jnp.where(condition, 1.0, 0.0).astype(jnp.bfloat16)

    same_z, same_y = zs == zt, ys == yt
    rank_az, many_az = count(flags, mask(same_z & (ys < yt))), count(flags, mask(same_z))
    rank_by, many_by = count(flags, mask(same_y & (zs < zt))), count(flags, mask(same_y))
    rank_ay, many_ay = count(mask(same_y & (zt < zs)), flags), count(mask(same_y), flags)
    rank_bz, many_bz = count(mask(same_z & (yt < ys)), flags), count(mask(same_z), flags)
    many_z, many_y = jnp.maximum(many_az, many_bz), jnp.maximum(many_ay, many_by)
    counts_z = [total_of(along_z == k, many_z) for k in range(1, 8)]
    counts_y = [total_of(along_y == k, many_y) for k in range(1, 4)]
    split_z, need_z = long_share(counts_z)
    split_y, need_y = short_share(counts_y)
    first_az, last_az = long_plan(counts_z, split_z, along_z, rank_az)
    first_bz, last_bz = long_plan(counts_z, split_z, along_z, rank_bz)
    first_ay, last_ay = short_plan(counts_y, split_y, along_y, rank_ay)
    first_by, last_by = short_plan(counts_y, split_y, along_y, rank_by)

    lanes = iota2((1, 64), 1)
    diagonal = source == target

    def standing(row):
        return jnp.sum(jnp.where(diagonal, row, 0), axis=1, keepdims=True)

    def table(place, values):
        at, value = standing(place), standing(values)
        return jnp.sum(jnp.where(at == lanes, value + 1, 0), axis=0, keepdims=True) - 1

    def own_row(values):
        return jnp.sum(jnp.where(source == me, values, 0), axis=0, keepdims=True)

    my_y, my_z = me >> 3, me & 7
    rows = []
    place = own_row(jnp.where(present & (along_z > 0), first_az, -1))
    rows += [table(place, own_row(held[p])) for p in range(2)]
    place = own_row(jnp.where(present & (along_y > 0), first_by, -1))
    rows += [table(place, own_row(held[p])) for p in range(2)]

    spread_y, spread_z = mask(ys == yt), mask(zs == zt)

    def condense(keep, values, spread, pick):
        moved = count(jnp.where(keep, values, 0).astype(jnp.float32).astype(jnp.bfloat16), spread)
        return jnp.sum(jnp.where(pick, moved, 0), axis=0, keepdims=True)

    keep = present & (along_y > 0) & (ys == my_y) & (zt == my_z)
    pick = (ys == my_y) & (zs == zt)
    place = condense(keep, first_ay + 1, spread_y, pick) - 1
    for p in range(2):
        code = jnp.where(along_z == 0, held[p], 32 + last_az)
        rows.append(table(place, condense(keep, code, spread_y, pick)))
    keep = present & (along_z > 0) & (zs == my_z) & (yt == my_y)
    pick = (zs == my_z) & (ys == yt)
    place = condense(keep, first_bz + 1, spread_z, pick) - 1
    for p in range(2):
        code = jnp.where(along_y == 0, held[p], 32 + last_by)
        rows.append(table(place, condense(keep, code, spread_z, pick)))

    def column(values):
        return jnp.sum(jnp.where(target == me, values, 0), axis=1, keepdims=True)

    for first_axis, second_axis, last_one, last_two in ((along_z, along_y, last_az, last_ay), (along_y, along_z, last_by, last_bz)):
        row = jnp.zeros((1, 64), jnp.int32)
        for p in range(2):
            code = jnp.where(
                second_axis > 0,
                160 + 2 * last_two + p,
                jnp.where(first_axis > 0, 32 + 2 * last_one + p, held[p]),
            )
            at, value = column(jnp.where(present, label[p] + 1, 0)) - 1, column(code)
            row = row + jnp.sum(jnp.where(at == lanes, value, 0), axis=0, keepdims=True)
        rows.append(row)
    return rows, need_z, need_y


MESH = pl.DeviceIdType.MESH
BUILDS = ((12, 8), (12, 9), (14, 8), (14, 9), (14, 11), (16, 11), (20, 12), (32, 16))


def along(axis, distance):
    dp = lax.axis_index("dp")
    if axis == "z":
        return ((dp // 8) * 8 + (dp + distance) % 8, lax.axis_index("mp"))
    return ((dp + 8 * distance) % 32, lax.axis_index("mp"))


def meet(devices):
    barrier = pltpu.get_barrier_semaphore()
    for device in devices:
        pl.semaphore_signal(barrier, inc=1, device_id=device, device_id_type=MESH)
    pl.semaphore_wait(barrier, len(devices))


def plan_kernel(slots_ref, table_ref, build_ref, owner, send_sem, recv_sem):
    dp = lax.axis_index("dp")
    row = dp // 8
    ring_z = [along("z", k) for k in range(1, 8)]
    ring_y = [along("y", k) for k in range(1, 4)]
    owner[pl.ds(dp, 1), :, 0 : slots_ref.shape[2]] = slots_ref[...]
    meet(ring_z + ring_y)
    copies = []
    for k, device in enumerate(ring_z):
        copies.append(
            pltpu.make_async_remote_copy(
                src_ref=owner.at[pl.ds(dp, 1)],
                dst_ref=owner.at[pl.ds(dp, 1)],
                send_sem=send_sem.at[k],
                recv_sem=recv_sem.at[k],
                device_id=device,
                device_id_type=MESH,
            )
        )
        copies[-1].start()
    for copy in copies:
        copy.wait_recv()
    for k, device in enumerate(ring_y):
        copies.append(
            pltpu.make_async_remote_copy(
                src_ref=owner.at[pl.ds(8 * row, 8)],
                dst_ref=owner.at[pl.ds(8 * row, 8)],
                send_sem=send_sem.at[7 + k],
                recv_sem=recv_sem.at[7 + k],
                device_id=device,
                device_id_type=MESH,
            )
        )
        copies[-1].start()
    for copy in copies[7:]:
        copy.wait_recv()
    for copy in copies:
        copy.wait_send()
    rows, need_z, need_y = plan(owner[...].reshape(32, 128), dp)
    for k, entries in enumerate(rows):
        table_ref[k : k + 1, 0:64] = entries
    build = jnp.full((1, 1), len(BUILDS) - 1, jnp.int32)
    for number in range(len(BUILDS) - 2, -1, -1):
        steps_z, steps_y = BUILDS[number]
        build = jnp.where((need_z <= steps_z) & (need_y <= steps_y), number, build)
    build_ref[...] = build


def make_plan(owner_slot):
    slots = owner_slot.reshape(1, 1, owner_slot.shape[0])
    vmem = pl.BlockSpec(memory_space=pltpu.VMEM)
    return pl.pallas_call(
        plan_kernel,
        out_shape=[jax.ShapeDtypeStruct((16, 128), jnp.int32), jax.ShapeDtypeStruct((1, 1), jnp.int32)],
        in_specs=[vmem],
        out_specs=[vmem, vmem],
        scratch_shapes=[
            pltpu.VMEM((32, 1, 128), jnp.int32),
            pltpu.SemaphoreType.DMA((10,)),
            pltpu.SemaphoreType.DMA((10,)),
        ],
        compiler_params=pltpu.CompilerParams(collective_id=0, has_side_effects=True),
        name="plan",
    )(slots)


class Lanes:
    def __init__(self, near, steps, rows, columns, table, own, before, buffers, sems):
        self.near, self.length, self.half = near
        self.steps, self.rows, self.columns = steps, rows, columns
        self.table, self.own, self.before = table, own, before
        self.sent, self.got = buffers
        self.send_sem, self.recv_sem = sems

    def received(self, entry, columns):
        unused = jnp.where(entry >= 2 * self.half, 2 * (self.half - self.steps), 0)
        return self.got[jnp.clip(entry - unused, 0, 4 * self.steps - 1), :, columns]

    def value(self, way, at, p, step):
        code = self.table[self.rows + p, way * self.half + at]
        fresh = self.own[jnp.clip(code, 0, 23), :, self.columns]
        if self.before is not None:
            lanes, columns = self.before
            fresh = jnp.where(code < 32, fresh, lanes.received(2 * (code - 32) + p, columns))
        if step == 0:
            return fresh
        return jnp.where(code >= 0, fresh, self.got[2 * (way * self.steps + at - 1) + p])

    def copy(self, way, at):
        plus, minus = self.near
        place = way * self.steps + at
        return pltpu.make_async_remote_copy(
            src_ref=self.sent.at[pl.ds(2 * place, 2)],
            dst_ref=self.got.at[pl.ds(2 * place, 2)],
            send_sem=self.send_sem.at[0],
            recv_sem=self.recv_sem.at[place],
            device_id=(plus + way * (minus - plus), lax.axis_index("mp")),
            device_id_type=MESH,
        )

    def each(self, step, action):
        lanes = (self.steps - step + self.length - 1) // self.length

        def body(number, carry):
            action(number % 2, number // 2 * self.length + step)
            return carry

        lax.fori_loop(0, 2 * lanes, body, 0)

    def fill(self, way, at, step):
        for p in range(2):
            self.sent[2 * (way * self.steps + at) + p] = self.value(way, at, p, step)

    def ready(self):
        self.each(0, lambda way, at: self.fill(way, at, 0))

    def leave(self):
        self.each(0, lambda way, at: self.copy(way, at).start())

    def step(self, step):
        def action(way, at):
            if step > 0:
                self.copy(way, at - 1).wait_recv()
            self.fill(way, at, step)
            self.copy(way, at).start()

        self.each(step, action)

    def arrive(self):
        whole, part = self.steps // self.length, self.steps % self.length

        def body(number, carry):
            lane = number // 2
            last = jnp.where(lane < whole, self.length, part) - 1
            self.copy(number % 2, lane * self.length + last).wait_recv()
            return carry

        lax.fori_loop(0, 2 * (whole + (part > 0)), body, 0)

    def close(self):
        pltpu.make_async_remote_copy(
            src_ref=self.sent,
            dst_ref=self.got,
            send_sem=self.send_sem.at[0],
            recv_sem=self.recv_sem.at[0],
            device_id=(self.near[0], lax.axis_index("mp")),
            device_id_type=MESH,
        ).wait_send()


def exchange_kernel(steps_z, steps_y, table, grads, blocks, own, *scratch):
    buffers_by = scratch[0:2]
    buffers_az, buffers_ay, buffers_bz = ((scratch[k : k + 2], scratch[k + 2 : k + 4]) for k in (2, 6, 10))
    packs = scratch[14]
    sems = [(scratch[15 + 2 * k], scratch[16 + 2 * k]) for k in range(7)]
    mp_send, mp_recv, local_sem = scratch[29:]
    mp = lax.axis_index("mp")
    dp = lax.axis_index("dp")
    load = pltpu.make_async_copy(grads, own, local_sem.at[4])
    load.start()
    barrier = pltpu.get_barrier_semaphore()
    row = (dp // 8) * 8
    near_z = (row + (dp + 1) % 8, row + (dp + 7) % 8)
    near_y = ((dp + 8) % 32, (dp + 24) % 32)
    for device in near_z + near_y:
        pl.semaphore_signal(barrier, inc=1, device_id=(device, mp), device_id_type=MESH)

    def greet(k, carry):
        pl.semaphore_signal(barrier, inc=1, device_id=(dp, (mp + k) % 8), device_id_type=MESH)
        return carry

    lax.fori_loop(1, 8, greet, 0)
    half = own.shape[2] // 2
    quarter = half // 2
    quarters = [pl.ds(k * quarter, quarter) for k in range(4)]
    by = Lanes((near_y, 2, 16), steps_y, 2, pl.ds(half, half), table, own, None, buffers_by, sems[0])
    az1, az2 = (
        Lanes((near_z, 4, 32), steps_z, 0, quarters[k], table, own, None, buffers_az[k], sems[1 + k])
        for k in range(2)
    )
    ay1, ay2 = (
        Lanes((near_y, 2, 16), steps_y, 4, quarters[k], table, own, ((az1, az2)[k], quarters[0]), buffers_ay[k], sems[3 + k])
        for k in range(2)
    )
    bz1, bz2 = (
        Lanes((near_z, 4, 32), steps_z, 6, quarters[2 + k], table, own, (by, quarters[k]), buffers_bz[k], sems[5 + k])
        for k in range(2)
    )
    load.wait()
    az1.ready()
    pl.semaphore_wait(barrier, 11)

    def place(number):
        return blocks.at[:, pl.ds(pl.multiple_of(64 * mp, 64), 64), quarters[number]]

    def spread(number, k):
        peer = (mp + k) % 8
        return pltpu.make_async_remote_copy(
            src_ref=packs.at[number, pl.ds(3 * peer, 3)],
            dst_ref=place(number),
            send_sem=mp_send.at[number],
            recv_sem=mp_recv.at[number, k],
            device_id=(dp, peer),
            device_id_type=MESH,
        )

    def keep(number):
        return pltpu.make_async_copy(packs.at[number, pl.ds(3 * mp, 3)], place(number), local_sem.at[number])

    def deliver(row, number, lanes):
        columns = quarters[number]
        first, first_columns = lanes.before

        def sort(peer):
            for k in range(3):
                slot = 3 * peer + k
                code = table[row, slot]
                packs[number, slot] = jnp.where(
                    code < 32,
                    own[jnp.clip(code, 0, 23), :, columns],
                    jnp.where(
                        code < 160,
                        first.received(code - 32, first_columns),
                        lanes.received(code - 160, quarters[0]),
                    ),
                )

        def send(k, carry):
            sort((mp + k) % 8)
            spread(number, k).start()
            return carry

        lax.fori_loop(1, 8, send, 0)
        sort(mp)
        keep(number).start()

    az1.leave()
    az2.step(0)
    by.step(0)
    az1.step(1)
    az2.step(1)
    by.step(1)
    az1.step(2)
    az2.step(2)
    az1.step(3)
    az2.step(3)
    by.arrive()
    bz1.step(0)
    az1.arrive()
    ay1.step(0)
    bz2.step(0)
    az2.arrive()
    ay1.step(1)
    ay2.step(0)
    bz1.step(1)
    bz2.step(1)
    ay1.arrive()
    deliver(8, 0, ay1)
    ay2.step(1)
    bz1.step(2)
    bz2.step(2)
    ay2.arrive()
    deliver(8, 1, ay2)
    bz1.step(3)
    bz2.step(3)
    bz1.arrive()
    deliver(9, 2, bz1)
    bz2.arrive()
    deliver(9, 3, bz2)
    for number in range(4):

        def settle(k, carry):
            spread(number, k).wait_recv()
            return carry

        lax.fori_loop(1, 8, settle, 0)
        pltpu.make_async_remote_copy(
            src_ref=packs.at[number, pl.ds(0, 21)],
            dst_ref=packs.at[number, pl.ds(0, 21)],
            send_sem=mp_send.at[number],
            recv_sem=mp_recv.at[number, 1],
            device_id=(dp, (mp + 1) % 8),
            device_id_type=MESH,
        ).wait_send()
        keep(number).wait()
    for lanes in (by, az1, az2, ay1, ay2, bz1, bz2):
        lanes.close()


def exchange(number, table, grads):
    steps_z, steps_y = BUILDS[number]
    held, rows, columns = grads.shape

    def buffers(steps, parts):
        return [pltpu.VMEM((4 * steps, rows, columns // parts), jnp.bfloat16)] * 2

    def sems(*steps):
        return [pltpu.SemaphoreType.DMA((size,)) for count in steps for size in (1, 2 * count)]

    return pl.pallas_call(
        functools.partial(exchange_kernel, steps_z, steps_y),
        out_shape=jax.ShapeDtypeStruct((3, columns, columns), jnp.bfloat16),
        in_specs=[pl.BlockSpec(memory_space=pltpu.SMEM), pl.BlockSpec(memory_space=pl.ANY)],
        out_specs=pl.BlockSpec(memory_space=pl.ANY),
        scratch_shapes=[pltpu.VMEM(grads.shape, jnp.bfloat16)]
        + buffers(steps_y, 2)
        + buffers(steps_z, 4) * 2
        + buffers(steps_y, 4) * 2
        + buffers(steps_z, 4) * 2
        + [pltpu.VMEM((4, held, rows, columns // 4), jnp.bfloat16)]
        + sems(steps_y, steps_z, steps_z, steps_y, steps_y, steps_z, steps_z)
        + [pltpu.SemaphoreType.DMA((4,)), pltpu.SemaphoreType.DMA((4, 8)), pltpu.SemaphoreType.DMA((5,))],
        compiler_params=pltpu.CompilerParams(
            collective_id=1 + number, has_side_effects=True, vmem_limit_bytes=56 << 20
        ),
        name=f"exchange_{steps_z}_{steps_y}",
    )(table, grads)


def newton_roots(*matrices):
    size = matrices[0].shape[0]
    diagonal = lax.broadcasted_iota(jnp.int32, (size, size), 0) == lax.broadcasted_iota(jnp.int32, (size, size), 1)

    def narrow(values):
        return [value.astype(jnp.bfloat16) for value in values]

    def products(first_ops, second_ops):
        return [multiply(one, two) for one, two in zip(first_ops, second_ops)]

    wide = [matrix.astype(jnp.float32) for matrix in matrices]
    scalings = [2.5 / jnp.sqrt(jnp.sum(value * value) + 1e-06) for value in wide]
    scaled = [scaling * value for scaling, value in zip(scalings, wide)]
    squared = [(scaling * scaling) * value for scaling, value in zip(scalings, products(matrices, matrices))]
    shift = [(two - 10.0 * one) * 0.0625 for one, two in zip(scaled, squared)]
    through = [(5.0 * one - two) * 0.25 for one, two in zip(scaled, squared)]
    half_shift = narrow(shift)
    quartic = [3.125 * one + two for one, two in zip(shift, products(half_shift, half_shift))]
    fifth = [2.44140625 * one + two for one, two in zip(through, products(narrow(quartic), narrow(through)))]
    offset = [-0.3125 * one - 0.25 * two for one, two in zip(scaled, fifth)]
    half_offset = narrow(offset)
    doubled = [3.125 * one + two for one, two in zip(offset, products(half_offset, half_offset))]
    half_doubled = narrow(doubled)
    carried = [
        1.5625 * one + scaling * two for scaling, one, two in zip(scalings, scaled, products(half_offset, matrices))
    ]
    fourth = [4.8828125 * one + two for one, two in zip(doubled, products(half_doubled, half_doubled))]
    last = [5.9604644775390625 * one + two for one, two in zip(carried, products(narrow(fourth), narrow(carried)))]
    return [
        (jnp.sqrt(jnp.sqrt(scaling)) * (jnp.where(diagonal, 1.953125, 0.0) + 1.25 * one - 0.25 * two)).astype(jnp.bfloat16)
        for scaling, one, two in zip(scalings, offset, last)
    ]


def update_kernel(flag_ref, grad_ref, left_ref, right_ref, left_root_ref, right_root_ref, left_out, right_out, dir_out, use_left, use_right):
    slot = pl.program_id(0)
    block = grad_ref[0]
    gram_left = lax.dot_general(block, block, (((1,), (1,)), ((), ())), preferred_element_type=jnp.float32)
    left_out[0] = (decay_rate * left_ref[0].astype(jnp.float32) + (1.0 - decay_rate) * gram_left).astype(jnp.bfloat16)
    gram_right = lax.dot_general(block, block, (((0,), (0,)), ((), ())), preferred_element_type=jnp.float32)
    right_out[0] = (decay_rate * right_ref[0].astype(jnp.float32) + (1.0 - decay_rate) * gram_right).astype(jnp.bfloat16)

    @pl.when(flag_ref[slot] > 0)
    def _():
        use_left[...], use_right[...] = newton_roots(left_out[0], right_out[0])

    @pl.when(flag_ref[slot] <= 0)
    def _():
        use_left[...] = left_root_ref[0]
        use_right[...] = right_root_ref[0]

    half_way = multiply(use_left[...], block).astype(jnp.bfloat16)
    preconditioned = multiply(half_way, use_right[...])
    wide = block.astype(jnp.float32)
    grad_norm = jnp.sum(wide * wide)
    dir_norm = jnp.sum(preconditioned * preconditioned)
    dir_out[0] = (preconditioned * jnp.sqrt(grad_norm / (dir_norm + 1e-06))).astype(jnp.bfloat16)


def update(refresh_flag, blocks, left_stats, right_stats, left_root, right_root):
    slots, size = blocks.shape[0], blocks.shape[1]
    spec = pl.BlockSpec((1, size, size), lambda k: (k, 0, 0))
    return pl.pallas_call(
        update_kernel,
        grid=(slots,),
        in_specs=[pl.BlockSpec(memory_space=pltpu.SMEM)] + [spec] * 5,
        out_specs=[spec] * 3,
        out_shape=[jax.ShapeDtypeStruct(blocks.shape, jnp.bfloat16)] * 3,
        scratch_shapes=[pltpu.VMEM((size, size), jnp.bfloat16)] * 2,
        compiler_params=pltpu.CompilerParams(vmem_limit_bytes=56 << 20),
        name="update",
    )(refresh_flag, blocks, left_stats, right_stats, left_root, right_root)


def local(grads, owner_slot, refresh_flag, left_stats, right_stats, left_root, right_root):
    table, build = make_plan(owner_slot)
    builds = [functools.partial(exchange, number) for number in range(len(BUILDS))]
    blocks = lax.switch(build[0, 0], builds, table, grads)
    return tuple(update(refresh_flag, blocks, left_stats, right_stats, left_root, right_root))


def solution(mesh):
    placed = (
        P("dp", "mp", None),
        P("dp"),
        P(("dp", "mp")),
        P(("dp", "mp"), None, None),
        P(("dp", "mp"), None, None),
        P(("dp", "mp"), None, None),
        P(("dp", "mp"), None, None),
    )
    return jax.shard_map(
        local,
        mesh=mesh,
        in_specs=placed,
        out_specs=(
            P(("dp", "mp"), None, None),
            P(("dp", "mp"), None, None),
            P(("dp", "mp"), None, None),
        ),
        check_vma=False,
    )
```
